256 devices in a mesh: frame: 32 (over x_hi, z, core), head: 8 (over x_lo, y).
Axes of the slice: x: 4 (x_hi: 2, x_lo: 2; x = x_hi * 2 + x_lo), y: 4, z: 8, core: 2. Of those that a mesh axis runs over, the one named last changes fastest.
Arguments:
- queries: bfloat16 [40960, 3072], P(('frame', 'head')), may hold values from -16 to 16
- keys: bfloat16 [40960, 3072], P(('frame', 'head')), may hold values from -16 to 16
- values: bfloat16 [40960, 3072], P(('frame', 'head')), may hold values from -6 to 6
- head_reach: int32 [24, 3], replicated, may hold values from 0 to 1, as said below
- frame_valid: int32 [32], replicated, may hold values from 0 to 1, as said below
Outputs:
- attended: bfloat16 [40960, 3072], P(('frame', 'head'))
The draws below stay inside these ranges and needn't reach their ends.
Inputs may be any that keep to these rules, and one draw needn't show every extreme that they name: `head_reach`: column 0 is a time reach in frames and takes every value 0 to 1 on some head; columns 1 and 2 are tile reaches and take both 0 and 1 on some head. `frame_valid`: 1 on a leading run of at least half of the 32 frames and 0 after it; the last frame is always 0.
All inputs are finite; a program needn't handle non-finite values.
Results may differ from the reference program's by a relative error of at most 0.006.
Values may be sent and summed in bfloat16 or wider, within the bound.
A program may use at most 128 MiB of HBM per device.

```python
import jax
import jax.numpy as jnp
from jax import lax

HEADS = 24
DH = 128
D = 3072
TILE = 8
TH_TILES = 2
TW_TILES = 10
TREACH = 1
FRAMES = 32
TOKENS = 40960


def draw_queries(key, part):
    key = jax.random.fold_in(key, 11)
    return jnp.clip(jax.random.normal(key, (TOKENS, D), jnp.float32), -4.0, 4.0).astype(jnp.bfloat16)


def draw_keys(key, part):
    key = jax.random.fold_in(key, 13)
    return jnp.clip(jax.random.normal(key, (TOKENS, D), jnp.float32), -4.0, 4.0).astype(jnp.bfloat16)


def draw_head_reach(key, part):
    key = jax.random.fold_in(key, 17)
    first = jax.random.permutation(jax.random.fold_in(key, 1), HEADS) % (TREACH + 1)
    second = jax.random.permutation(jax.random.fold_in(key, 2), HEADS) % 2
    third = jax.random.permutation(jax.random.fold_in(key, 3), HEADS) % 2
    return jnp.stack([first, second, third], axis=1).astype(jnp.int32)


def draw_frame_valid(key, part):
    key = jax.random.fold_in(key, 19)
    count = jax.random.randint(key, (), FRAMES // 2, FRAMES)
    return (jnp.arange(FRAMES) < count).astype(jnp.int32)


def levels(stream_key, dims, split, low, high):
    factor_of = 1.0
    for axis_at, shards_of in split:
        steps = jax.random.uniform(jax.random.fold_in(jax.random.fold_in(stream_key, 6), axis_at), (shards_of,), jnp.float32, low / len(split), high / len(split))
        factor_of = factor_of * jnp.repeat(jnp.exp(steps), dims[axis_at] // shards_of).reshape((-1,) + (1,) * (len(dims) - 1 - axis_at))
    return factor_of


def gaussian(stream_key, extent, scale, bound, split=(), held_as=jnp.bfloat16):
    array = scale * jax.random.normal(stream_key, extent, jnp.float32)
    if split:
        array = array * levels(stream_key, extent, split, -0.22, 0.18)
    return jnp.clip(array, -bound, bound).astype(held_as)


def setup_inputs(seed: int = 0) -> dict:
    splits = jax.random.split(jax.random.key(seed), 6)
    queries = draw_queries(jax.random.fold_in(splits[5], 71), 0)
    keys = draw_keys(jax.random.fold_in(splits[5], 71), 0)
    values = gaussian(splits[2], (TOKENS, D), 1.0, 6.0, ((0, 256),))
    head_reach = draw_head_reach(jax.random.fold_in(splits[5], 71), 0)
    frame_valid = draw_frame_valid(jax.random.fold_in(splits[5], 71), 0)
    return dict(queries=queries, keys=keys, values=values, head_reach=head_reach, frame_valid=frame_valid)


def window_mask(reach, live, pos):
    row_width = TW_TILES * TILE
    tile_y = (pos // row_width) // TILE
    tile_x = (pos % row_width) // TILE

    def bounds(tile, span_reach, count):
        size = jnp.minimum(2 * span_reach + 1, count)
        start = jnp.clip(tile - span_reach, 0, count - size)
        return start, start + size

    low_y, high_y = bounds(tile_y, reach[1], TH_TILES)
    low_x, high_x = bounds(tile_x, reach[2], TW_TILES)
    spatial = (tile_y[None, :] >= low_y[:, None]) & (tile_y[None, :] < high_y[:, None])
    spatial = spatial & (tile_x[None, :] >= low_x[:, None]) & (tile_x[None, :] < high_x[:, None])
    offsets = jnp.arange(2 * TREACH + 1) - TREACH
    timely = (jnp.abs(offsets) <= reach[0]) & (live > 0)
    joined = timely[None, :, None] & spatial[:, None, :]
    return joined.reshape(pos.shape[0], -1)


def reference(queries, keys, values, head_reach, frame_valid):
    frame_tokens = TH_TILES * TW_TILES * TILE * TILE
    span = 2 * TREACH + 1
    scale = DH ** -0.5
    query_grid = queries.reshape(FRAMES, frame_tokens, HEADS, DH)
    key_grid = jnp.pad(keys.reshape(FRAMES, frame_tokens, HEADS, DH), ((TREACH, TREACH), (0, 0), (0, 0), (0, 0)))
    value_grid = jnp.pad(values.reshape(FRAMES, frame_tokens, HEADS, DH), ((TREACH, TREACH), (0, 0), (0, 0), (0, 0)))
    live_pad = jnp.pad(frame_valid, (TREACH, TREACH))
    pos = jnp.arange(frame_tokens)

    def per_head(head):
        reach = head_reach[head]

        def per_frame(frame):
            query = lax.dynamic_index_in_dim(query_grid[:, :, head, :], frame, 0, False)
            near_k = lax.dynamic_slice_in_dim(key_grid[:, :, head, :], frame, span, 0).reshape(span * frame_tokens, DH)
            near_v = lax.dynamic_slice_in_dim(value_grid[:, :, head, :], frame, span, 0).reshape(span * frame_tokens, DH)
            live = lax.dynamic_slice_in_dim(live_pad, frame, span, 0)
            mask = window_mask(reach, live, pos)
            scores = jnp.dot(query, near_k.T, preferred_element_type=jnp.float32) * scale
            scores = jnp.where(mask, scores, jnp.float32(-1e30))
            top = jnp.max(scores, axis=1, keepdims=True)
            weights = jnp.where(mask, jnp.exp(scores - top), jnp.float32(0.0)).astype(jnp.bfloat16)
            total = jnp.sum(weights.astype(jnp.float32), axis=1, keepdims=True)
            mixed = jnp.dot(weights, near_v, preferred_element_type=jnp.float32) / total
            keep = lax.dynamic_index_in_dim(frame_valid, frame, 0, False) > 0
            return jnp.where(keep, mixed, jnp.float32(0.0)).astype(jnp.bfloat16)

        return lax.map(per_frame, jnp.arange(FRAMES))

    result = lax.map(per_head, jnp.arange(HEADS))
    return jnp.transpose(result, (1, 2, 0, 3)).reshape(TOKENS, D)
```

```python
import functools
import math

import jax
import jax.numpy as jnp
from jax import lax
from jax.experimental import pallas as pl
from jax.experimental.pallas import tpu as pltpu
from jax.sharding import PartitionSpec as P

DH = 128
ROWS = 2
PAIRS = 5
PIX = 16
TW = 10
LOCAL = 3
VMEM = 64 * 2**20
MESH = pl.DeviceIdType.MESH
BIG = float(2**20)
SCALE = math.log2(math.e) / math.sqrt(DH)


def query_features(pair, reach_h, reach_w):
    shape = (8 * ROWS * PIX, DH)
    row = lax.broadcasted_iota(jnp.int32, shape, 0)
    col = lax.broadcasted_iota(jnp.int32, shape, 1)
    tile_y = row >> 7
    tile_x = 2 * pair + ((row & 15) >> 3)
    key_y = (col >= TW).astype(jnp.int32)
    key_x = col - TW * key_y
    size_y = jnp.minimum(2 * reach_h + 1, 2)
    size_x = jnp.minimum(2 * reach_w + 1, TW)
    low_y = jnp.clip(tile_y - reach_h, 0, 2 - size_y)
    low_x = jnp.clip(tile_x - reach_w, 0, TW - size_x)
    inside = (key_y >= low_y) & (key_y < low_y + size_y)
    inside = inside & (key_x >= low_x) & (key_x < low_x + size_x)
    return jnp.where(inside, jnp.float32(0.0), jnp.float32(-BIG))


def key_features(part, pair):
    shape = (ROWS, PIX, DH)
    pix = lax.broadcasted_iota(jnp.int32, shape, 1)
    col = lax.broadcasted_iota(jnp.int32, shape, 2)
    tile = (part // 4) * TW + 2 * pair + (pix >> 3)
    return jnp.where(col == tile, jnp.float32(1.0), jnp.float32(0.0)).astype(jnp.bfloat16)


def wait_bytes(ref, sem):
    pltpu.make_async_copy(ref, ref, sem).wait()


def kernel(
    frames, reach_hbm, valid_hbm, q_ref, k_ref, v_ref, out_ref,
    qbuf, kvbuf, kfeat, obuf, reach_ref, valid_ref,
    send_sem, in_sem, fwd_sem, halo_sem, out_send_sem, out_sem, small_sem,
):
    frame = lax.axis_index("frame")
    me = lax.axis_index("head")
    half = frames // 2

    def swap(index, at):
        return lax.rem(index + jnp.where(at >= half, 4, 0), 8)

    group = swap(me, frame)
    has_prev = frame > 0
    has_next = frame < frames - 1
    prev_id = {"frame": frame - 1, "head": swap(group, frame - 1)}
    next_id = {"frame": frame + 1, "head": swap(group, frame + 1)}

    def peer(step):
        part = lax.rem(me // 4 + step // 4, 2) * 4 + lax.rem(me + step, 4)
        return part

    barrier = pltpu.get_barrier_semaphore()
    for step in range(1, 8):
        pl.semaphore_signal(
            barrier, inc=1, device_id={"frame": frame, "head": peer(step)}, device_id_type=MESH
        )

    @pl.when(has_prev)
    def _():
        pl.semaphore_signal(barrier, inc=1, device_id=prev_id, device_id_type=MESH)

    @pl.when(has_next)
    def _():
        pl.semaphore_signal(barrier, inc=1, device_id=next_id, device_id_type=MESH)

    pl.semaphore_wait(
        barrier, 7 + jnp.where(has_prev, 1, 0) + jnp.where(has_next, 1, 0)
    )

    def cols(of_group, head):
        return pl.ds(pl.multiple_of((of_group * LOCAL + head) * DH, DH), DH)

    order = (5, 1, 4, 3, 6, 2, 7)

    def send_head(head):
        for at, ref in ((1, k_ref), (2, v_ref), (0, q_ref)):
            land = qbuf.at[head, me] if at == 0 else kvbuf.at[at - 1, 1, head, me]
            for step in order:
                target = peer(step)
                pltpu.make_async_remote_copy(
                    src_ref=ref.at[:, :, :, cols(swap(target, frame), head)],
                    dst_ref=land,
                    send_sem=send_sem.at[at],
                    recv_sem=in_sem.at[at, head],
                    device_id={"frame": frame, "head": target},
                    device_id_type=MESH,
                ).start()
            pltpu.make_async_copy(
                ref.at[:, :, :, cols(group, head)], land, in_sem.at[at, head]
            ).start()

    for head in range(LOCAL):
        send_head(head)

    reach_copy = pltpu.make_async_copy(reach_hbm, reach_ref, small_sem.at[0])
    valid_copy = pltpu.make_async_copy(valid_hbm, valid_ref, small_sem.at[1])
    reach_copy.start()
    valid_copy.start()

    for part in range(8):
        for pair in range(PAIRS):
            kfeat[part, :, pair] = key_features(part, pair)

    @pl.when(jnp.logical_not(has_prev))
    def _():
        kvbuf[:, 0] = jnp.zeros(kvbuf.shape[:1] + kvbuf.shape[2:], jnp.bfloat16)

    @pl.when(jnp.logical_not(has_next))
    def _():
        kvbuf[:, 2] = jnp.zeros(kvbuf.shape[:1] + kvbuf.shape[2:], jnp.bfloat16)

    def forward(head, kv, way):
        return pltpu.make_async_remote_copy(
            src_ref=kvbuf.at[kv, 1, head],
            dst_ref=kvbuf.at[kv, 2 - 2 * way, head],
            send_sem=fwd_sem.at[kv, way, head],
            recv_sem=halo_sem.at[kv, way, head],
            device_id=(prev_id, next_id)[way],
            device_id_type=MESH,
        )

    def pass_on(head):
        for kv in range(2):
            wait_bytes(kvbuf.at[kv, 1, head], in_sem.at[kv + 1, head])

            @pl.when(has_prev)
            def _():
                forward(head, kv, 0).start()

            @pl.when(has_next)
            def _():
                forward(head, kv, 1).start()

    reach_copy.wait()
    valid_copy.wait()
    live_own = valid_ref[0, frame]
    live_prev = jnp.where(has_prev, valid_ref[0, jnp.maximum(frame - 1, 0)], 0)
    live_next = jnp.where(has_next, valid_ref[0, jnp.minimum(frame + 1, frames - 1)], 0)

    def attend(head, pair):
        row = group * LOCAL + head
        reach_t = reach_ref[0, row]
        base = query_features(pair, reach_ref[1, row], reach_ref[2, row])
        near = reach_t >= 1
        allowed = ((live_prev > 0) & near, live_own > 0, (live_next > 0) & near)
        query = qbuf[head, :, :, pair].reshape(8 * ROWS * PIX, DH)
        first, last = max(pair - 1, 0), min(pair + 2, PAIRS)
        count = 8 * ROWS * (last - first) * PIX
        tiles = kfeat[:, :, first:last].reshape(count, DH)
        scores = []
        for slot in range(3):
            features = jnp.minimum(
                base, jnp.where(allowed[slot], jnp.float32(0.0), jnp.float32(-BIG))
            ).astype(jnp.bfloat16)
            keys = kvbuf[0, slot, head, :, :, first:last].reshape(count, DH)
            scores.append(
                lax.dot_general(
                    jnp.concatenate([query, features], axis=1),
                    jnp.concatenate([keys, tiles], axis=1),
                    (((1,), (1,)), ((), ())),
                    preferred_element_type=jnp.float32,
                )
            )
        top = functools.reduce(jnp.maximum, [jnp.max(s, axis=1, keepdims=True) for s in scores])
        ones = jnp.ones((count, DH), jnp.bfloat16)
        mixed = None
        for slot in range(3):
            weights = jnp.exp2((scores[slot] - top) * SCALE).astype(jnp.bfloat16)
            values = kvbuf[1, slot, head, :, :, first:last].reshape(count, DH)
            term = jnp.dot(
                weights,
                jnp.concatenate([values, ones], axis=1),
                preferred_element_type=jnp.float32,
            )
            mixed = term if mixed is None else mixed + term
        result = mixed[:, :DH] / mixed[:, DH:]
        result = jnp.where(live_own > 0, result, jnp.float32(0.0)).astype(jnp.bfloat16)
        obuf[head, :, :, pair] = result.reshape(8, ROWS, PIX, DH)

    def send_out(head):
        for step in order:
            target = peer(step)
            pltpu.make_async_remote_copy(
                src_ref=obuf.at[head, target],
                dst_ref=out_ref.at[:, :, :, cols(group, head)],
                send_sem=out_send_sem,
                recv_sem=out_sem,
                device_id={"frame": frame, "head": target},
                device_id_type=MESH,
            ).start()
        pltpu.make_async_copy(
            obuf.at[head, me], out_ref.at[:, :, :, cols(group, head)], out_sem
        ).start()

    pass_on(0)

    def per_head(head, carry):
        @pl.when(head < LOCAL - 1)
        def _():
            pass_on(head + 1)

        wait_bytes(qbuf.at[head], in_sem.at[0, head])
        for kv in range(2):

            @pl.when(has_next)
            def _():
                forward(head, kv, 0).wait_recv()

            @pl.when(has_prev)
            def _():
                forward(head, kv, 1).wait_recv()

        for pair in range(PAIRS):
            attend(head, pair)
        send_out(head)
        return carry

    lax.fori_loop(0, LOCAL, per_head, 0)

    for at in range(3):
        wait_bytes(qbuf.at[:, 0:7], send_sem.at[at])
    for head in range(LOCAL):
        for kv in range(2):

            @pl.when(has_prev)
            def _():
                forward(head, kv, 0).wait_send()

            @pl.when(has_next)
            def _():
                forward(head, kv, 1).wait_send()

    wait_bytes(obuf.at[:, 0:7], out_send_sem)
    wait_bytes(obuf, out_sem)


def solution(mesh):
    frames = mesh.shape["frame"]
    block = (8, ROWS, PAIRS, PIX, DH)

    def body(queries, keys, values, head_reach, frame_valid):
        grid = (ROWS, PAIRS, PIX, queries.shape[1])
        hbm = pl.BlockSpec(memory_space=pltpu.HBM)
        out = pl.pallas_call(
            functools.partial(kernel, frames),
            out_shape=jax.ShapeDtypeStruct(grid, jnp.bfloat16),
            in_specs=[hbm] * 5,
            out_specs=hbm,
            scratch_shapes=[
                pltpu.VMEM((LOCAL,) + block, jnp.bfloat16),
                pltpu.VMEM((2, 3, LOCAL) + block, jnp.bfloat16),
                pltpu.VMEM(block, jnp.bfloat16),
                pltpu.VMEM((LOCAL,) + block, jnp.bfloat16),
                pltpu.SMEM((3, head_reach.shape[0]), jnp.int32),
                pltpu.SMEM((1, frames), jnp.int32),
                pltpu.SemaphoreType.DMA((3,)),
                pltpu.SemaphoreType.DMA((3, LOCAL)),
                pltpu.SemaphoreType.DMA((2, 2, LOCAL)),
                pltpu.SemaphoreType.DMA((2, 2, LOCAL)),
                pltpu.SemaphoreType.DMA,
                pltpu.SemaphoreType.DMA,
                pltpu.SemaphoreType.DMA((2,)),
            ],
            compiler_params=pltpu.CompilerParams(
                collective_id=0, has_side_effects=True, vmem_limit_bytes=VMEM
            ),
        )(
            head_reach.T,
            frame_valid.reshape(1, frames),
            queries.reshape(grid),
            keys.reshape(grid),
            values.reshape(grid),
        )
        return out.reshape(queries.shape)

    rows = P(("frame", "head"), None)
    return jax.shard_map(
        body, mesh=mesh, in_specs=(rows, rows, rows, P(), P()), out_specs=rows, check_vma=False
    )
```

```python
import functools
import math

import jax
import jax.numpy as jnp
from jax import lax
from jax.experimental import pallas as pl
from jax.experimental.pallas import tpu as pltpu
from jax.sharding import PartitionSpec as P

DH = 128
ROWS = 2
PAIRS = 5
PIX = 16
TW = 10
LOCAL = 3
VMEM = 62 * 2**20
MESH = pl.DeviceIdType.MESH
BIG = float(2**20)
SCALE = math.log2(math.e) / math.sqrt(DH)


def query_features(pair, reach_h, reach_w):
    shape = (8 * ROWS * PIX, DH)
    row = lax.broadcasted_iota(jnp.int32, shape, 0)
    col = lax.broadcasted_iota(jnp.int32, shape, 1)
    tile_y = row >> 7
    tile_x = 2 * pair + ((row & 15) >> 3)
    key_y = (col >= TW).astype(jnp.int32)
    key_x = col - TW * key_y
    size_y = jnp.minimum(2 * reach_h + 1, 2)
    size_x = jnp.minimum(2 * reach_w + 1, TW)
    low_y = jnp.clip(tile_y - reach_h, 0, 2 - size_y)
    low_x = jnp.clip(tile_x - reach_w, 0, TW - size_x)
    inside = (key_y >= low_y) & (key_y < low_y + size_y)
    inside = inside & (key_x >= low_x) & (key_x < low_x + size_x)
    return jnp.where(inside, jnp.float32(0.0), jnp.float32(-BIG))


def key_features(part, pair):
    shape = (ROWS, PIX, DH)
    pix = lax.broadcasted_iota(jnp.int32, shape, 1)
    col = lax.broadcasted_iota(jnp.int32, shape, 2)
    tile = (part // 4) * TW + 2 * pair + (pix >> 3)
    return jnp.where(col == tile, jnp.float32(1.0), jnp.float32(0.0)).astype(jnp.bfloat16)


def wait_bytes(ref, sem):
    pltpu.make_async_copy(ref, ref, sem).wait()


def kernel(
    frames, reach_hbm, valid_hbm, q_ref, k_ref, v_ref, out_ref,
    qbuf, kvbuf, kfeat, obuf, reach_ref, valid_ref,
    send_sem, in_sem, fwd_sem, halo_sem, out_send_sem, out_sem, small_sem,
):
    frame = lax.axis_index("frame")
    me = lax.axis_index("head")
    half = frames // 2

    def swap(index, at):
        return lax.rem(index + jnp.where(at >= half, 4, 0), 8)

    group = swap(me, frame)
    has_prev = frame > 0
    has_next = frame < frames - 1
    prev_id = {"frame": frame - 1, "head": swap(group, frame - 1)}
    next_id = {"frame": frame + 1, "head": swap(group, frame + 1)}

    def peer(step):
        part = lax.rem(me // 4 + step // 4, 2) * 4 + lax.rem(me + step, 4)
        return part

    barrier = pltpu.get_barrier_semaphore()
    for step in range(1, 8):
        pl.semaphore_signal(
            barrier, inc=1, device_id={"frame": frame, "head": peer(step)}, device_id_type=MESH
        )

    @pl.when(has_prev)
    def _():
        pl.semaphore_signal(barrier, inc=1, device_id=prev_id, device_id_type=MESH)

    @pl.when(has_next)
    def _():
        pl.semaphore_signal(barrier, inc=1, device_id=next_id, device_id_type=MESH)

    pl.semaphore_wait(
        barrier, 7 + jnp.where(has_prev, 1, 0) + jnp.where(has_next, 1, 0)
    )

    def cols(of_group, head):
        return pl.ds(pl.multiple_of((of_group * LOCAL + head) * DH, DH), DH)

    order = (5, 1, 4, 3, 6, 2, 7)

    def send(at, head):
        ref = (q_ref, k_ref, v_ref)[at]
        land = qbuf.at[head, me] if at == 0 else kvbuf.at[at - 1, 1, head, me]
        for step in order:
            target = peer(step)
            pltpu.make_async_remote_copy(
                src_ref=ref.at[:, :, :, cols(swap(target, frame), head)],
                dst_ref=land,
                send_sem=send_sem.at[at],
                recv_sem=in_sem.at[at, head],
                device_id={"frame": frame, "head": target},
                device_id_type=MESH,
            ).start()
        pltpu.make_async_copy(
            ref.at[:, :, :, cols(group, head)], land, in_sem.at[at, head]
        ).start()

    for at, head in ((1, 0), (2, 0), (0, 0), (1, 1), (2, 1), (1, 2), (2, 2), (0, 1), (0, 2)):
        send(at, head)

    reach_copy = pltpu.make_async_copy(reach_hbm, reach_ref, small_sem.at[0])
    valid_copy = pltpu.make_async_copy(valid_hbm, valid_ref, small_sem.at[1])
    reach_copy.start()
    valid_copy.start()

    for part in range(8):
        for pair in range(PAIRS):
            kfeat[part, :, pair] = key_features(part, pair)

    @pl.when(jnp.logical_not(has_prev))
    def _():
        kvbuf[:, 0] = jnp.zeros(kvbuf.shape[:1] + kvbuf.shape[2:], jnp.bfloat16)

    @pl.when(jnp.logical_not(has_next))
    def _():
        kvbuf[:, 2] = jnp.zeros(kvbuf.shape[:1] + kvbuf.shape[2:], jnp.bfloat16)

    def forward(head, kv, way):
        return pltpu.make_async_remote_copy(
            src_ref=kvbuf.at[kv, 1, head],
            dst_ref=kvbuf.at[kv, 2 - 2 * way, head],
            send_sem=fwd_sem.at[kv, way, head],
            recv_sem=halo_sem.at[kv, way, head],
            device_id=(prev_id, next_id)[way],
            device_id_type=MESH,
        )

    def pass_on(head):
        for kv in range(2):
            wait_bytes(kvbuf.at[kv, 1, head], in_sem.at[kv + 1, head])

            @pl.when(has_prev)
            def _():
                forward(head, kv, 0).start()

            @pl.when(has_next)
            def _():
                forward(head, kv, 1).start()

    reach_copy.wait()
    valid_copy.wait()
    live_own = valid_ref[0, frame]
    live_prev = jnp.where(has_prev, valid_ref[0, jnp.maximum(frame - 1, 0)], 0)
    live_next = jnp.where(has_next, valid_ref[0, jnp.minimum(frame + 1, frames - 1)], 0)

    def attend(head, pair):
        row = group * LOCAL + head
        reach_t = reach_ref[0, row]
        base = query_features(pair, reach_ref[1, row], reach_ref[2, row])
        near = reach_t >= 1
        allowed = ((live_prev > 0) & near, live_own > 0, (live_next > 0) & near)
        query = qbuf[head, :, :, pair].reshape(8 * ROWS * PIX, DH)
        first, last = max(pair - 1, 0), min(pair + 2, PAIRS)
        count = 8 * ROWS * (last - first) * PIX
        tiles = kfeat[:, :, first:last].reshape(count, DH)
        scores = []
        for slot in range(3):
            features = jnp.minimum(
                base, jnp.where(allowed[slot], jnp.float32(0.0), jnp.float32(-BIG))
            ).astype(jnp.bfloat16)
            keys = kvbuf[0, slot, head, :, :, first:last].reshape(count, DH)
            scores.append(
                lax.dot_general(
                    jnp.concatenate([query, features], axis=1),
                    jnp.concatenate([keys, tiles], axis=1),
                    (((1,), (1,)), ((), ())),
                    preferred_element_type=jnp.float32,
                )
            )
        top = functools.reduce(jnp.maximum, [jnp.max(s, axis=1, keepdims=True) for s in scores])
        ones = jnp.ones((count, DH), jnp.bfloat16)
        mixed = None
        for slot in range(3):
            weights = jnp.exp2((scores[slot] - top) * SCALE).astype(jnp.bfloat16)
            values = kvbuf[1, slot, head, :, :, first:last].reshape(count, DH)
            term = jnp.dot(
                weights,
                jnp.concatenate([values, ones], axis=1),
                preferred_element_type=jnp.float32,
            )
            mixed = term if mixed is None else mixed + term
        result = mixed[:, :DH] / mixed[:, DH:]
        result = jnp.where(live_own > 0, result, jnp.float32(0.0)).astype(jnp.bfloat16)
        obuf[head, :, :, pair] = result.reshape(8, ROWS, PIX, DH)

    def send_out(head, first, last):
        landing = out_ref.at[:, first:last, :, cols(group, head)]
        for step in order:
            target = peer(step)
            pltpu.make_async_remote_copy(
                src_ref=obuf.at[head, target, :, first:last],
                dst_ref=landing,
                send_sem=out_send_sem,
                recv_sem=out_sem,
                device_id={"frame": frame, "head": target},
                device_id_type=MESH,
            ).start()
        pltpu.make_async_copy(obuf.at[head, me, :, first:last], landing, out_sem).start()

    pass_on(0)

    def per_head(head, carry):
        @pl.when(head < LOCAL - 1)
        def _():
            pass_on(head + 1)

        wait_bytes(qbuf.at[head], in_sem.at[0, head])
        for kv in range(2):

            @pl.when(has_next)
            def _():
                forward(head, kv, 0).wait_recv()

            @pl.when(has_prev)
            def _():
                forward(head, kv, 1).wait_recv()

        for first, last in ((0, 3), (3, PAIRS)):
            for pair in range(first, last):
                attend(head, pair)
            send_out(head, first, last)
        return carry

    lax.fori_loop(0, LOCAL, per_head, 0)

    for at in range(3):
        wait_bytes(qbuf.at[:, 0:7], send_sem.at[at])
    for head in range(LOCAL):
        for kv in range(2):

            @pl.when(has_prev)
            def _():
                forward(head, kv, 0).wait_send()

            @pl.when(has_next)
            def _():
                forward(head, kv, 1).wait_send()

    wait_bytes(obuf.at[:, 0:7], out_send_sem)
    wait_bytes(obuf, out_sem)


def solution(mesh):
    frames = mesh.shape["frame"]
    block = (8, ROWS, PAIRS, PIX, DH)

    def body(queries, keys, values, head_reach, frame_valid):
        grid = (ROWS, PAIRS, PIX, queries.shape[1])
        hbm = pl.BlockSpec(memory_space=pltpu.HBM)
        out = pl.pallas_call(
            functools.partial(kernel, frames),
            out_shape=pltpu.VMEM(grid, jnp.bfloat16),
            in_specs=[hbm] * 5,
            out_specs=pl.BlockSpec(memory_space=pltpu.VMEM),
            scratch_shapes=[
                pltpu.VMEM((LOCAL,) + block, jnp.bfloat16),
                pltpu.VMEM((2, 3, LOCAL) + block, jnp.bfloat16),
                pltpu.VMEM(block, jnp.bfloat16),
                pltpu.VMEM((LOCAL,) + block, jnp.bfloat16),
                pltpu.SMEM((3, head_reach.shape[0]), jnp.int32),
                pltpu.SMEM((1, frames), jnp.int32),
                pltpu.SemaphoreType.DMA((3,)),
                pltpu.SemaphoreType.DMA((3, LOCAL)),
                pltpu.SemaphoreType.DMA((2, 2, LOCAL)),
                pltpu.SemaphoreType.DMA((2, 2, LOCAL)),
                pltpu.SemaphoreType.DMA,
                pltpu.SemaphoreType.DMA,
                pltpu.SemaphoreType.DMA((2,)),
            ],
            compiler_params=pltpu.CompilerParams(
                collective_id=0, has_side_effects=True, vmem_limit_bytes=VMEM
            ),
        )(
            head_reach.T,
            frame_valid.reshape(1, frames),
            *(
                pltpu.with_memory_space_constraint(array.reshape(grid), pltpu.HBM)
                for array in (queries, keys, values)
            ),
        )
        return out.reshape(queries.shape)

    rows = P(("frame", "head"), None)
    return jax.shard_map(
        body, mesh=mesh, in_specs=(rows, rows, rows, P(), P()), out_specs=rows, check_vma=False
    )
```

```python
import functools
import math

import jax
import jax.numpy as jnp
from jax import lax
from jax.experimental import pallas as pl
from jax.experimental.pallas import tpu as pltpu
from jax.sharding import PartitionSpec as P

DH = 128
ROWS = 2
PAIRS = 5
PIX = 16
TW = 10
LOCAL = 3
VMEM = 62 * 2**20
MESH = pl.DeviceIdType.MESH
BIG = float(2**20)
SCALE = math.log2(math.e) / math.sqrt(DH)


def query_features(pair, reach_h, reach_w):
    shape = (8 * ROWS * PIX, DH)
    row = lax.broadcasted_iota(jnp.int32, shape, 0)
    col = lax.broadcasted_iota(jnp.int32, shape, 1)
    tile_y = row >> 7
    tile_x = 2 * pair + ((row & 15) >> 3)
    key_y = (col >= TW).astype(jnp.int32)
    key_x = col - TW * key_y
    size_y = jnp.minimum(2 * reach_h + 1, 2)
    size_x = jnp.minimum(2 * reach_w + 1, TW)
    low_y = jnp.clip(tile_y - reach_h, 0, 2 - size_y)
    low_x = jnp.clip(tile_x - reach_w, 0, TW - size_x)
    inside = (key_y >= low_y) & (key_y < low_y + size_y)
    inside = inside & (key_x >= low_x) & (key_x < low_x + size_x)
    return jnp.where(inside, jnp.float32(0.0), jnp.float32(-BIG))


def key_features(part, pair):
    shape = (ROWS, PIX, DH)
    pix = lax.broadcasted_iota(jnp.int32, shape, 1)
    col = lax.broadcasted_iota(jnp.int32, shape, 2)
    tile = (part // 4) * TW + 2 * pair + (pix >> 3)
    return jnp.where(col == tile, jnp.float32(1.0), jnp.float32(0.0)).astype(jnp.bfloat16)


def wait_bytes(ref, sem):
    pltpu.make_async_copy(ref, ref, sem).wait()


def kernel(
    frames, reach_hbm, valid_hbm, q_ref, k_ref, v_ref, out_ref,
    qbuf, kvbuf, kfeat, obuf, reach_ref, valid_ref,
    send_sem, in_sem, fwd_sem, halo_sem, out_send_sem, out_sem, small_sem,
):
    frame = lax.axis_index("frame")
    me = lax.axis_index("head")
    half = frames // 2

    def swap(index, at):
        return lax.rem(index + jnp.where(at >= half, 4, 0), 8)

    group = swap(me, frame)
    has_prev = frame > 0
    has_next = frame < frames - 1
    prev_id = {"frame": frame - 1, "head": swap(group, frame - 1)}
    next_id = {"frame": frame + 1, "head": swap(group, frame + 1)}

    def peer(step):
        part = lax.rem(me // 4 + step // 4, 2) * 4 + lax.rem(me + step, 4)
        return part

    barrier = pltpu.get_barrier_semaphore()
    for step in range(1, 8):
        pl.semaphore_signal(
            barrier, inc=1, device_id={"frame": frame, "head": peer(step)}, device_id_type=MESH
        )

    @pl.when(has_prev)
    def _():
        pl.semaphore_signal(barrier, inc=1, device_id=prev_id, device_id_type=MESH)

    @pl.when(has_next)
    def _():
        pl.semaphore_signal(barrier, inc=1, device_id=next_id, device_id_type=MESH)

    pl.semaphore_wait(
        barrier, 7 + jnp.where(has_prev, 1, 0) + jnp.where(has_next, 1, 0)
    )

    def cols(of_group, head):
        return pl.ds(pl.multiple_of((of_group * LOCAL + head) * DH, DH), DH)

    order = (5, 1, 4, 3, 6, 2, 7)

    def send(at, head):
        ref = (q_ref, k_ref, v_ref)[at]
        land = qbuf.at[head, me] if at == 0 else kvbuf.at[at - 1, 1, head, me]
        for step in order:
            target = peer(step)
            pltpu.make_async_remote_copy(
                src_ref=ref.at[:, :, :, cols(swap(target, frame), head)],
                dst_ref=land,
                send_sem=send_sem.at[at],
                recv_sem=in_sem.at[at, head],
                device_id={"frame": frame, "head": target},
                device_id_type=MESH,
            ).start()
        pltpu.make_async_copy(
            ref.at[:, :, :, cols(group, head)], land, in_sem.at[at, head]
        ).start()

    for at, head in ((1, 0), (2, 0), (0, 0), (1, 1), (2, 1), (0, 1), (1, 2), (2, 2), (0, 2)):
        send(at, head)

    reach_copy = pltpu.make_async_copy(reach_hbm, reach_ref, small_sem.at[0])
    valid_copy = pltpu.make_async_copy(valid_hbm, valid_ref, small_sem.at[1])
    reach_copy.start()
    valid_copy.start()

    for part in range(8):
        for pair in range(PAIRS):
            kfeat[part, :, pair] = key_features(part, pair)

    @pl.when(jnp.logical_not(has_prev))
    def _():
        kvbuf[:, 0] = jnp.zeros(kvbuf.shape[:1] + kvbuf.shape[2:], jnp.bfloat16)

    @pl.when(jnp.logical_not(has_next))
    def _():
        kvbuf[:, 2] = jnp.zeros(kvbuf.shape[:1] + kvbuf.shape[2:], jnp.bfloat16)

    def forward(head, kv, way):
        return pltpu.make_async_remote_copy(
            src_ref=kvbuf.at[kv, 1, head],
            dst_ref=kvbuf.at[kv, 2 - 2 * way, head],
            send_sem=fwd_sem.at[kv, way, head],
            recv_sem=halo_sem.at[kv, way, head],
            device_id=(prev_id, next_id)[way],
            device_id_type=MESH,
        )

    def pass_on(head):
        for kv in range(2):
            wait_bytes(kvbuf.at[kv, 1, head], in_sem.at[kv + 1, head])

            @pl.when(has_prev)
            def _():
                forward(head, kv, 0).start()

            @pl.when(has_next)
            def _():
                forward(head, kv, 1).start()

    reach_copy.wait()
    valid_copy.wait()
    live_own = valid_ref[0, frame]
    live_prev = jnp.where(has_prev, valid_ref[0, jnp.maximum(frame - 1, 0)], 0)
    live_next = jnp.where(has_next, valid_ref[0, jnp.minimum(frame + 1, frames - 1)], 0)

    def attend(head, pair):
        row = group * LOCAL + head
        reach_t = reach_ref[0, row]
        base = query_features(pair, reach_ref[1, row], reach_ref[2, row])
        near = reach_t >= 1
        allowed = ((live_prev > 0) & near, live_own > 0, (live_next > 0) & near)
        query = qbuf[head, :, :, pair].reshape(8 * ROWS * PIX, DH)
        first, last = max(pair - 1, 0), min(pair + 2, PAIRS)
        count = 8 * ROWS * (last - first) * PIX
        tiles = kfeat[:, :, first:last].reshape(count, DH)
        scores = []
        for slot in range(3):
            features = jnp.minimum(
                base, jnp.where(allowed[slot], jnp.float32(0.0), jnp.float32(-BIG))
            ).astype(jnp.bfloat16)
            keys = kvbuf[0, slot, head, :, :, first:last].reshape(count, DH)
            scores.append(
                lax.dot_general(
                    jnp.concatenate([query, features], axis=1),
                    jnp.concatenate([keys, tiles], axis=1),
                    (((1,), (1,)), ((), ())),
                    preferred_element_type=jnp.float32,
                )
            )
        top = functools.reduce(jnp.maximum, [jnp.max(s, axis=1, keepdims=True) for s in scores])
        ones = jnp.ones((count, DH), jnp.bfloat16)
        mixed = None
        for slot in range(3):
            weights = jnp.exp2((scores[slot] - top) * SCALE).astype(jnp.bfloat16)
            values = kvbuf[1, slot, head, :, :, first:last].reshape(count, DH)
            term = jnp.dot(
                weights,
                jnp.concatenate([values, ones], axis=1),
                preferred_element_type=jnp.float32,
            )
            mixed = term if mixed is None else mixed + term
        result = mixed[:, :DH] / mixed[:, DH:]
        result = jnp.where(live_own > 0, result, jnp.float32(0.0)).astype(jnp.bfloat16)
        obuf[head, :, :, pair] = result.reshape(8, ROWS, PIX, DH)

    def send_out(head, first, last):
        landing = out_ref.at[:, first:last, :, cols(group, head)]
        for step in order:
            target = peer(step)
            pltpu.make_async_remote_copy(
                src_ref=obuf.at[head, target, :, first:last],
                dst_ref=landing,
                send_sem=out_send_sem,
                recv_sem=out_sem,
                device_id={"frame": frame, "head": target},
                device_id_type=MESH,
            ).start()
        pltpu.make_async_copy(obuf.at[head, me, :, first:last], landing, out_sem).start()

    def per_head(head, carry):
        pass_on(head)
        wait_bytes(qbuf.at[head], in_sem.at[0, head])
        last_head = head == LOCAL - 1

        @pl.when(last_head)
        def _():
            for done in range(LOCAL - 1):
                send_out(done, 0, PAIRS)

        for kv in range(2):

            @pl.when(has_next)
            def _():
                forward(head, kv, 0).wait_recv()

            @pl.when(has_prev)
            def _():
                forward(head, kv, 1).wait_recv()

        for first, last in ((0, 2), (2, 4), (4, PAIRS)):
            for pair in range(first, last):
                attend(head, pair)

            @pl.when(last_head)
            def _():
                send_out(head, first, last)

        return carry

    lax.fori_loop(0, LOCAL, per_head, 0)

    for at in range(3):
        wait_bytes(qbuf.at[:, 0:7], send_sem.at[at])
    for head in range(LOCAL):
        for kv in range(2):

            @pl.when(has_prev)
            def _():
                forward(head, kv, 0).wait_send()

            @pl.when(has_next)
            def _():
                forward(head, kv, 1).wait_send()

    wait_bytes(obuf.at[:, 0:7], out_send_sem)
    wait_bytes(obuf, out_sem)


def solution(mesh):
    frames = mesh.shape["frame"]
    block = (8, ROWS, PAIRS, PIX, DH)

    def body(queries, keys, values, head_reach, frame_valid):
        grid = (ROWS, PAIRS, PIX, queries.shape[1])
        hbm = pl.BlockSpec(memory_space=pltpu.HBM)
        out = pl.pallas_call(
            functools.partial(kernel, frames),
            out_shape=pltpu.VMEM(grid, jnp.bfloat16),
            in_specs=[hbm] * 5,
            out_specs=pl.BlockSpec(memory_space=pltpu.VMEM),
            scratch_shapes=[
                pltpu.VMEM((LOCAL,) + block, jnp.bfloat16),
                pltpu.VMEM((2, 3, LOCAL) + block, jnp.bfloat16),
                pltpu.VMEM(block, jnp.bfloat16),
                pltpu.VMEM((LOCAL,) + block, jnp.bfloat16),
                pltpu.SMEM((3, head_reach.shape[0]), jnp.int32),
                pltpu.SMEM((1, frames), jnp.int32),
                pltpu.SemaphoreType.DMA((3,)),
                pltpu.SemaphoreType.DMA((3, LOCAL)),
                pltpu.SemaphoreType.DMA((2, 2, LOCAL)),
                pltpu.SemaphoreType.DMA((2, 2, LOCAL)),
                pltpu.SemaphoreType.DMA,
                pltpu.SemaphoreType.DMA,
                pltpu.SemaphoreType.DMA((2,)),
            ],
            compiler_params=pltpu.CompilerParams(
                collective_id=0, has_side_effects=True, vmem_limit_bytes=VMEM
            ),
        )(
            head_reach.T,
            frame_valid.reshape(1, frames),
            *(
                pltpu.with_memory_space_constraint(array.reshape(grid), pltpu.HBM)
                for array in (queries, keys, values)
            ),
        )
        return out.reshape(queries.shape)

    rows = P(("frame", "head"), None)
    return jax.shard_map(
        body, mesh=mesh, in_specs=(rows, rows, rows, P(), P()), out_specs=rows, check_vma=False
    )
```

```python
import functools
import math

import jax
import jax.numpy as jnp
from jax import lax
from jax.experimental import pallas as pl
from jax.experimental.pallas import tpu as pltpu
from jax.sharding import PartitionSpec as P

DH = 128
ROWS = 2
PAIRS = 5
PIX = 16
TW = 10
LOCAL = 3
VMEM = 62 * 2**20
MESH = pl.DeviceIdType.MESH
BIG = float(2**20)
SCALE = math.log2(math.e) / math.sqrt(DH)


def query_features(pair, reach_h, reach_w):
    shape = (8 * ROWS * PIX, DH)
    row = lax.broadcasted_iota(jnp.int32, shape, 0)
    col = lax.broadcasted_iota(jnp.int32, shape, 1)
    tile_y = row >> 7
    tile_x = 2 * pair + ((row & 15) >> 3)
    key_y = (col >= TW).astype(jnp.int32)
    key_x = col - TW * key_y
    size_y = jnp.minimum(2 * reach_h + 1, 2)
    size_x = jnp.minimum(2 * reach_w + 1, TW)
    low_y = jnp.clip(tile_y - reach_h, 0, 2 - size_y)
    low_x = jnp.clip(tile_x - reach_w, 0, TW - size_x)
    inside = (key_y >= low_y) & (key_y < low_y + size_y)
    inside = inside & (key_x >= low_x) & (key_x < low_x + size_x)
    return jnp.where(inside, jnp.float32(0.0), jnp.float32(-BIG))


def key_features(part, pair):
    shape = (ROWS, PIX, DH)
    pix = lax.broadcasted_iota(jnp.int32, shape, 1)
    col = lax.broadcasted_iota(jnp.int32, shape, 2)
    tile = (part // 4) * TW + 2 * pair + (pix >> 3)
    return jnp.where(col == tile, jnp.float32(1.0), jnp.float32(0.0)).astype(jnp.bfloat16)


def wait_bytes(ref, sem):
    pltpu.make_async_copy(ref, ref, sem).wait()


def kernel(
    frames, reach_hbm, valid_hbm, q_ref, k_ref, v_ref, out_ref,
    qbuf, kvbuf, kfeat, obuf, reach_ref, valid_ref,
    send_sem, in_sem, fwd_sem, halo_sem, out_send_sem, out_sem, small_sem,
):
    frame = lax.axis_index("frame")
    me = lax.axis_index("head")
    half = frames // 2

    def swap(index, at):
        return lax.rem(index + jnp.where(at >= half, 4, 0), 8)

    group = swap(me, frame)
    has_prev = frame > 0
    has_next = frame < frames - 1
    prev_id = {"frame": frame - 1, "head": swap(group, frame - 1)}
    next_id = {"frame": frame + 1, "head": swap(group, frame + 1)}

    def peer(step):
        part = lax.rem(me // 4 + step // 4, 2) * 4 + lax.rem(me + step, 4)
        return part

    barrier = pltpu.get_barrier_semaphore()
    for step in range(1, 8):
        pl.semaphore_signal(
            barrier, inc=1, device_id={"frame": frame, "head": peer(step)}, device_id_type=MESH
        )

    @pl.when(has_prev)
    def _():
        pl.semaphore_signal(barrier, inc=1, device_id=prev_id, device_id_type=MESH)

    @pl.when(has_next)
    def _():
        pl.semaphore_signal(barrier, inc=1, device_id=next_id, device_id_type=MESH)

    pl.semaphore_wait(
        barrier, 7 + jnp.where(has_prev, 1, 0) + jnp.where(has_next, 1, 0)
    )

    def cols(of_group, head):
        return pl.ds(pl.multiple_of((of_group * LOCAL + head) * DH, DH), DH)

    order = (5, 1, 4, 3, 6, 2, 7)

    def send(at, head):
        ref = (q_ref, k_ref, v_ref)[at]
        land = qbuf.at[head, me] if at == 0 else kvbuf.at[at - 1, 1, head, me]
        for step in order:
            target = peer(step)
            pltpu.make_async_remote_copy(
                src_ref=ref.at[:, :, :, cols(swap(target, frame), head)],
                dst_ref=land,
                send_sem=send_sem.at[at],
                recv_sem=in_sem.at[at, head],
                device_id={"frame": frame, "head": target},
                device_id_type=MESH,
            ).start()
        pltpu.make_async_copy(
            ref.at[:, :, :, cols(group, head)], land, in_sem.at[at, head]
        ).start()

    for at, head in ((1, 0), (2, 0), (0, 0), (1, 1), (2, 1), (0, 1), (1, 2), (2, 2), (0, 2)):
        send(at, head)

    reach_copy = pltpu.make_async_copy(reach_hbm, reach_ref, small_sem.at[0])
    valid_copy = pltpu.make_async_copy(valid_hbm, valid_ref, small_sem.at[1])
    reach_copy.start()
    valid_copy.start()

    for part in range(8):
        for pair in range(PAIRS):
            kfeat[part, :, pair] = key_features(part, pair)

    @pl.when(jnp.logical_not(has_prev))
    def _():
        kvbuf[:, 0] = jnp.zeros(kvbuf.shape[:1] + kvbuf.shape[2:], jnp.bfloat16)

    @pl.when(jnp.logical_not(has_next))
    def _():
        kvbuf[:, 2] = jnp.zeros(kvbuf.shape[:1] + kvbuf.shape[2:], jnp.bfloat16)

    def forward(head, kv, way):
        return pltpu.make_async_remote_copy(
            src_ref=kvbuf.at[kv, 1, head],
            dst_ref=kvbuf.at[kv, 2 - 2 * way, head],
            send_sem=fwd_sem.at[kv, way, head],
            recv_sem=halo_sem.at[kv, way, head],
            device_id=(prev_id, next_id)[way],
            device_id_type=MESH,
        )

    def pass_on(head, kv):
        wait_bytes(kvbuf.at[kv, 1, head], in_sem.at[kv + 1, head])

        @pl.when(has_prev)
        def _():
            forward(head, kv, 0).start()

        @pl.when(has_next)
        def _():
            forward(head, kv, 1).start()

    reach_copy.wait()
    valid_copy.wait()
    live_own = valid_ref[0, frame]
    live_prev = jnp.where(has_prev, valid_ref[0, jnp.maximum(frame - 1, 0)], 0)
    live_next = jnp.where(has_next, valid_ref[0, jnp.minimum(frame + 1, frames - 1)], 0)

    def attend(head, pair):
        row = group * LOCAL + head
        reach_t = reach_ref[0, row]
        base = query_features(pair, reach_ref[1, row], reach_ref[2, row])
        near = reach_t >= 1
        allowed = ((live_prev > 0) & near, live_own > 0, (live_next > 0) & near)
        query = qbuf[head, :, :, pair].reshape(8 * ROWS * PIX, DH)
        first, last = max(pair - 1, 0), min(pair + 2, PAIRS)
        count = 8 * ROWS * (last - first) * PIX
        tiles = kfeat[:, :, first:last].reshape(count, DH)
        scores = []
        for slot in range(3):
            features = jnp.minimum(
                base, jnp.where(allowed[slot], jnp.float32(0.0), jnp.float32(-BIG))
            ).astype(jnp.bfloat16)
            keys = kvbuf[0, slot, head, :, :, first:last].reshape(count, DH)
            scores.append(
                lax.dot_general(
                    jnp.concatenate([query, features], axis=1),
                    jnp.concatenate([keys, tiles], axis=1),
                    (((1,), (1,)), ((), ())),
                    preferred_element_type=jnp.float32,
                )
            )
        top = functools.reduce(jnp.maximum, [jnp.max(s, axis=1, keepdims=True) for s in scores])
        ones = jnp.ones((count, DH), jnp.bfloat16)
        mixed = None
        for slot in range(3):
            weights = jnp.exp2((scores[slot] - top) * SCALE).astype(jnp.bfloat16)
            values = kvbuf[1, slot, head, :, :, first:last].reshape(count, DH)
            term = jnp.dot(
                weights,
                jnp.concatenate([values, ones], axis=1),
                preferred_element_type=jnp.float32,
            )
            mixed = term if mixed is None else mixed + term
        result = mixed[:, :DH] / mixed[:, DH:]
        result = jnp.where(live_own > 0, result, jnp.float32(0.0)).astype(jnp.bfloat16)
        obuf[head, :, :, pair] = result.reshape(8, ROWS, PIX, DH)

    def send_out(head, first, last):
        landing = out_ref.at[:, first:last, :, cols(group, head)]
        for step in order:
            target = peer(step)
            pltpu.make_async_remote_copy(
                src_ref=obuf.at[head, target, :, first:last],
                dst_ref=landing,
                send_sem=out_send_sem,
                recv_sem=out_sem,
                device_id={"frame": frame, "head": target},
                device_id_type=MESH,
            ).start()
        pltpu.make_async_copy(obuf.at[head, me, :, first:last], landing, out_sem).start()

    pass_on(0, 0)
    pass_on(0, 1)

    def per_head(head, carry):
        last_head = head == LOCAL - 1
        wait_bytes(qbuf.at[head], in_sem.at[0, head])

        @pl.when(last_head)
        def _():
            for done in range(LOCAL - 1):
                send_out(done, 0, PAIRS)

        for kv in range(2):

            @pl.when(has_next)
            def _():
                forward(head, kv, 0).wait_recv()

            @pl.when(has_prev)
            def _():
                forward(head, kv, 1).wait_recv()

        for first, last, kv in ((0, 2, 0), (2, 4, None), (4, PAIRS, 1)):
            for pair in range(first, last):
                attend(head, pair)

            @pl.when(last_head)
            def _():
                send_out(head, first, last)

            if kv is not None:

                @pl.when(jnp.logical_not(last_head))
                def _():
                    pass_on(head + 1, kv)

        return carry

    lax.fori_loop(0, LOCAL, per_head, 0)

    for at in range(3):
        wait_bytes(qbuf.at[:, 0:7], send_sem.at[at])
    for head in range(LOCAL):
        for kv in range(2):

            @pl.when(has_prev)
            def _():
                forward(head, kv, 0).wait_send()

            @pl.when(has_next)
            def _():
                forward(head, kv, 1).wait_send()

    wait_bytes(obuf.at[:, 0:7], out_send_sem)
    wait_bytes(obuf, out_sem)


def solution(mesh):
    frames = mesh.shape["frame"]
    block = (8, ROWS, PAIRS, PIX, DH)

    def body(queries, keys, values, head_reach, frame_valid):
        grid = (ROWS, PAIRS, PIX, queries.shape[1])
        hbm = pl.BlockSpec(memory_space=pltpu.HBM)
        out = pl.pallas_call(
            functools.partial(kernel, frames),
            out_shape=pltpu.VMEM(grid, jnp.bfloat16),
            in_specs=[hbm] * 5,
            out_specs=pl.BlockSpec(memory_space=pltpu.VMEM),
            scratch_shapes=[
                pltpu.VMEM((LOCAL,) + block, jnp.bfloat16),
                pltpu.VMEM((2, 3, LOCAL) + block, jnp.bfloat16),
                pltpu.VMEM(block, jnp.bfloat16),
                pltpu.VMEM((LOCAL,) + block, jnp.bfloat16),
                pltpu.SMEM((3, head_reach.shape[0]), jnp.int32),
                pltpu.SMEM((1, frames), jnp.int32),
                pltpu.SemaphoreType.DMA((3,)),
                pltpu.SemaphoreType.DMA((3, LOCAL)),
                pltpu.SemaphoreType.DMA((2, 2, LOCAL)),
                pltpu.SemaphoreType.DMA((2, 2, LOCAL)),
                pltpu.SemaphoreType.DMA,
                pltpu.SemaphoreType.DMA,
                pltpu.SemaphoreType.DMA((2,)),
            ],
            compiler_params=pltpu.CompilerParams(
                collective_id=0, has_side_effects=True, vmem_limit_bytes=VMEM
            ),
        )(
            head_reach.T,
            frame_valid.reshape(1, frames),
            *(
                pltpu.with_memory_space_constraint(array.reshape(grid), pltpu.HBM)
                for array in (queries, keys, values)
            ),
        )
        return out.reshape(queries.shape)

    rows = P(("frame", "head"), None)
    return jax.shard_map(
        body, mesh=mesh, in_specs=(rows, rows, rows, P(), P()), out_specs=rows, check_vma=False
    )
```

```python
import functools
import math

import jax
import jax.numpy as jnp
from jax import lax
from jax.experimental import pallas as pl
from jax.experimental.pallas import tpu as pltpu
from jax.sharding import PartitionSpec as P

DH = 128
ROWS = 2
PAIRS = 5
PIX = 16
TW = 10
LOCAL = 3
BLOCK = 8 * ROWS * PIX
VMEM = 62 * 2**20
MESH = pl.DeviceIdType.MESH
BIG = float(2**20)
SCALE = math.log2(math.e) / math.sqrt(DH)


def query_features(pair, reach_h, reach_w):
    shape = (BLOCK, DH)
    row = lax.broadcasted_iota(jnp.int32, shape, 0)
    col = lax.broadcasted_iota(jnp.int32, shape, 1)
    tile_y = row >> 7
    tile_x = 2 * pair + ((row & 15) >> 3)
    key_y = (col >= TW).astype(jnp.int32)
    key_x = col - TW * key_y
    size_y = jnp.minimum(2 * reach_h + 1, 2)
    size_x = jnp.minimum(2 * reach_w + 1, TW)
    low_y = jnp.clip(tile_y - reach_h, 0, 2 - size_y)
    low_x = jnp.clip(tile_x - reach_w, 0, TW - size_x)
    inside = (key_y >= low_y) & (key_y < low_y + size_y)
    inside = inside & (key_x >= low_x) & (key_x < low_x + size_x)
    return jnp.where(inside, jnp.float32(0.0), jnp.float32(-BIG))


def key_features(part, pair):
    shape = (ROWS, PIX, DH)
    pix = lax.broadcasted_iota(jnp.int32, shape, 1)
    col = lax.broadcasted_iota(jnp.int32, shape, 2)
    tile = (part // 4) * TW + 2 * pair + (pix >> 3)
    return jnp.where(col == tile, jnp.float32(1.0), jnp.float32(0.0)).astype(jnp.bfloat16)


def wait_bytes(ref, sem):
    pltpu.make_async_copy(ref, ref, sem).wait()


def kernel(
    frames, reach_hbm, valid_hbm, q_ref, k_ref, v_ref, out_ref,
    qbuf, kvbuf, kfeat, vturn, obuf, reach_ref, valid_ref,
    send_sem, in_sem, fwd_sem, halo_sem, out_send_sem, out_sem, small_sem,
):
    frame = lax.axis_index("frame")
    me = lax.axis_index("head")
    half = frames // 2

    def swap(index, at):
        return lax.rem(index + jnp.where(at >= half, 4, 0), 8)

    group = swap(me, frame)
    has_prev = frame > 0
    has_next = frame < frames - 1
    prev_id = {"frame": frame - 1, "head": swap(group, frame - 1)}
    next_id = {"frame": frame + 1, "head": swap(group, frame + 1)}

    def peer(step):
        part = lax.rem(me // 4 + step // 4, 2) * 4 + lax.rem(me + step, 4)
        return part

    barrier = pltpu.get_barrier_semaphore()
    for step in range(1, 8):
        pl.semaphore_signal(
            barrier, inc=1, device_id={"frame": frame, "head": peer(step)}, device_id_type=MESH
        )

    @pl.when(has_prev)
    def _():
        pl.semaphore_signal(barrier, inc=1, device_id=prev_id, device_id_type=MESH)

    @pl.when(has_next)
    def _():
        pl.semaphore_signal(barrier, inc=1, device_id=next_id, device_id_type=MESH)

    pl.semaphore_wait(
        barrier, 7 + jnp.where(has_prev, 1, 0) + jnp.where(has_next, 1, 0)
    )

    def cols(of_group, head):
        return pl.ds(pl.multiple_of((of_group * LOCAL + head) * DH, DH), DH)

    order = (5, 1, 4, 3, 6, 2, 7)

    def send(at, head):
        ref = (q_ref, k_ref, v_ref)[at]
        land = qbuf.at[head, me] if at == 0 else kvbuf.at[at - 1, 1, head, me]
        for step in order:
            target = peer(step)
            pltpu.make_async_remote_copy(
                src_ref=ref.at[:, :, :, cols(swap(target, frame), head)],
                dst_ref=land,
                send_sem=send_sem.at[at],
                recv_sem=in_sem.at[at, head],
                device_id={"frame": frame, "head": target},
                device_id_type=MESH,
            ).start()
        pltpu.make_async_copy(
            ref.at[:, :, :, cols(group, head)], land, in_sem.at[at, head]
        ).start()

    for at, head in ((1, 0), (2, 0), (0, 0), (1, 1), (2, 1), (1, 2), (2, 2), (0, 1), (0, 2)):
        send(at, head)

    reach_copy = pltpu.make_async_copy(reach_hbm, reach_ref, small_sem.at[0])
    valid_copy = pltpu.make_async_copy(valid_hbm, valid_ref, small_sem.at[1])
    reach_copy.start()
    valid_copy.start()

    for part in range(8):
        for pair in range(PAIRS):
            kfeat[part, :, pair] = key_features(part, pair)

    vturn[:, DH:] = jnp.ones((3, 16, PAIRS * BLOCK), jnp.bfloat16)

    @pl.when(jnp.logical_not(has_prev))
    def _():
        kvbuf[:, 0] = jnp.zeros(kvbuf.shape[:1] + kvbuf.shape[2:], jnp.bfloat16)

    @pl.when(jnp.logical_not(has_next))
    def _():
        kvbuf[:, 2] = jnp.zeros(kvbuf.shape[:1] + kvbuf.shape[2:], jnp.bfloat16)

    def forward(head, kv, way):
        return pltpu.make_async_remote_copy(
            src_ref=kvbuf.at[kv, 1, head],
            dst_ref=kvbuf.at[kv, 2 - 2 * way, head],
            send_sem=fwd_sem.at[kv, way, head],
            recv_sem=halo_sem.at[kv, way, head],
            device_id=(prev_id, next_id)[way],
            device_id_type=MESH,
        )

    def pass_on(head):
        for kv in range(2):
            wait_bytes(kvbuf.at[kv, 1, head], in_sem.at[kv + 1, head])

            @pl.when(has_prev)
            def _():
                forward(head, kv, 0).start()

            @pl.when(has_next)
            def _():
                forward(head, kv, 1).start()

    reach_copy.wait()
    valid_copy.wait()
    live_own = valid_ref[0, frame]
    live_prev = jnp.where(has_prev, valid_ref[0, jnp.maximum(frame - 1, 0)], 0)
    live_next = jnp.where(has_next, valid_ref[0, jnp.minimum(frame + 1, frames - 1)], 0)

    def turn_values(head):
        for slot in range(3):
            for pair in range(PAIRS):
                values = kvbuf[1, slot, head, :, :, pair].reshape(BLOCK, DH)
                vturn[slot, :DH, pair * BLOCK : (pair + 1) * BLOCK] = values.T

    def attend(head, pair):
        row = group * LOCAL + head
        base = query_features(pair, reach_ref[1, row], reach_ref[2, row])
        near = reach_ref[0, row] >= 1
        allowed = ((live_prev > 0) & near, live_own > 0, (live_next > 0) & near)
        query = qbuf[head, :, :, pair].reshape(BLOCK, DH)
        first, last = max(pair - 1, 0), min(pair + 2, PAIRS)
        scores = []
        for slot in range(3):
            features = jnp.minimum(
                base, jnp.where(allowed[slot], jnp.float32(0.0), jnp.float32(-BIG))
            ).astype(jnp.bfloat16)
            stationary = jnp.concatenate([query, features], axis=1)
            for at in range(first, last):
                keys = kvbuf[0, slot, head, :, :, at].reshape(BLOCK, DH)
                tiles = kfeat[:, :, at].reshape(BLOCK, DH)
                scores.append(
                    lax.dot_general(
                        jnp.concatenate([keys, tiles], axis=1),
                        stationary,
                        (((1,), (1,)), ((), ())),
                        preferred_element_type=jnp.float32,
                    )
                )
        top = jnp.max(functools.reduce(jnp.maximum, scores), axis=0, keepdims=True)
        weights = jnp.concatenate(
            [jnp.exp2((s - top) * SCALE).astype(jnp.bfloat16) for s in scores], axis=0
        )
        turned = jnp.concatenate(
            [vturn[slot, :, first * BLOCK : last * BLOCK] for slot in range(3)], axis=1
        )
        mixed = jnp.dot(turned, weights, preferred_element_type=jnp.float32)
        result = mixed[:DH] / mixed[DH : DH + 1]
        result = jnp.where(live_own > 0, result, jnp.float32(0.0)).T.astype(jnp.bfloat16)
        obuf[head, :, :, pair] = result.reshape(8, ROWS, PIX, DH)

    def send_out(head, first, last):
        landing = out_ref.at[:, first:last, :, cols(group, head)]
        for step in order:
            target = peer(step)
            pltpu.make_async_remote_copy(
                src_ref=obuf.at[head, target, :, first:last],
                dst_ref=landing,
                send_sem=out_send_sem,
                recv_sem=out_sem,
                device_id={"frame": frame, "head": target},
                device_id_type=MESH,
            ).start()
        pltpu.make_async_copy(obuf.at[head, me, :, first:last], landing, out_sem).start()

    pass_on(0)

    def per_head(head, carry):
        @pl.when(head < LOCAL - 1)
        def _():
            pass_on(head + 1)

        wait_bytes(qbuf.at[head], in_sem.at[0, head])
        for kv in range(2):

            @pl.when(has_next)
            def _():
                forward(head, kv, 0).wait_recv()

            @pl.when(has_prev)
            def _():
                forward(head, kv, 1).wait_recv()

        turn_values(head)
        for first, last in ((0, 3), (3, PAIRS)):
            for pair in range(first, last):
                attend(head, pair)
            send_out(head, first, last)
        return carry

    lax.fori_loop(0, LOCAL, per_head, 0)

    for at in range(3):
        wait_bytes(qbuf.at[:, 0:7], send_sem.at[at])
    for head in range(LOCAL):
        for kv in range(2):

            @pl.when(has_prev)
            def _():
                forward(head, kv, 0).wait_send()

            @pl.when(has_next)
            def _():
                forward(head, kv, 1).wait_send()

    wait_bytes(obuf.at[:, 0:7], out_send_sem)
    wait_bytes(obuf, out_sem)


def solution(mesh):
    frames = mesh.shape["frame"]
    block = (8, ROWS, PAIRS, PIX, DH)

    def body(queries, keys, values, head_reach, frame_valid):
        grid = (ROWS, PAIRS, PIX, queries.shape[1])
        hbm = pl.BlockSpec(memory_space=pltpu.HBM)
        out = pl.pallas_call(
            functools.partial(kernel, frames),
            out_shape=pltpu.VMEM(grid, jnp.bfloat16),
            in_specs=[hbm] * 5,
            out_specs=pl.BlockSpec(memory_space=pltpu.VMEM),
            scratch_shapes=[
                pltpu.VMEM((LOCAL,) + block, jnp.bfloat16),
                pltpu.VMEM((2, 3, LOCAL) + block, jnp.bfloat16),
                pltpu.VMEM(block, jnp.bfloat16),
                pltpu.VMEM((3, DH + 16, PAIRS * BLOCK), jnp.bfloat16),
                pltpu.VMEM((LOCAL,) + block, jnp.bfloat16),
                pltpu.SMEM((3, head_reach.shape[0]), jnp.int32),
                pltpu.SMEM((1, frames), jnp.int32),
                pltpu.SemaphoreType.DMA((3,)),
                pltpu.SemaphoreType.DMA((3, LOCAL)),
                pltpu.SemaphoreType.DMA((2, 2, LOCAL)),
                pltpu.SemaphoreType.DMA((2, 2, LOCAL)),
                pltpu.SemaphoreType.DMA,
                pltpu.SemaphoreType.DMA,
                pltpu.SemaphoreType.DMA((2,)),
            ],
            compiler_params=pltpu.CompilerParams(
                collective_id=0, has_side_effects=True, vmem_limit_bytes=VMEM
            ),
        )(
            head_reach.T,
            frame_valid.reshape(1, frames),
            *(
                pltpu.with_memory_space_constraint(array.reshape(grid), pltpu.HBM)
                for array in (queries, keys, values)
            ),
        )
        return out.reshape(queries.shape)

    rows = P(("frame", "head"), None)
    return jax.shard_map(
        body, mesh=mesh, in_specs=(rows, rows, rows, P(), P()), out_specs=rows, check_vma=False
    )
```

```python
import functools
import math

import jax
import jax.numpy as jnp
from jax import lax
from jax.experimental import pallas as pl
from jax.experimental.pallas import tpu as pltpu
from jax.sharding import PartitionSpec as P

DH = 128
ROWS = 2
PAIRS = 5
PIX = 16
TW = 10
LOCAL = 3
BLOCK = 8 * ROWS * PIX
VMEM = 62 * 2**20
MESH = pl.DeviceIdType.MESH
BIG = float(2**20)
SCALE = math.log2(math.e) / math.sqrt(DH)


def query_features(pair, reach_h, reach_w):
    shape = (DH, BLOCK)
    row = lax.broadcasted_iota(jnp.int32, shape, 1)
    col = lax.broadcasted_iota(jnp.int32, shape, 0)
    tile_y = row >> 7
    tile_x = 2 * pair + ((row & 15) >> 3)
    key_y = (col >= TW).astype(jnp.int32)
    key_x = col - TW * key_y
    size_y = jnp.minimum(2 * reach_h + 1, 2)
    size_x = jnp.minimum(2 * reach_w + 1, TW)
    low_y = jnp.clip(tile_y - reach_h, 0, 2 - size_y)
    low_x = jnp.clip(tile_x - reach_w, 0, TW - size_x)
    inside = (key_y >= low_y) & (key_y < low_y + size_y)
    inside = inside & (key_x >= low_x) & (key_x < low_x + size_x)
    return jnp.where(inside, jnp.float32(0.0), jnp.float32(-BIG))


def key_features(part, pair):
    shape = (ROWS, PIX, DH)
    pix = lax.broadcasted_iota(jnp.int32, shape, 1)
    col = lax.broadcasted_iota(jnp.int32, shape, 2)
    tile = (part // 4) * TW + 2 * pair + (pix >> 3)
    return jnp.where(col == tile, jnp.float32(1.0), jnp.float32(0.0)).astype(jnp.bfloat16)


def wait_bytes(ref, sem):
    pltpu.make_async_copy(ref, ref, sem).wait()


def kernel(
    frames, reach_hbm, valid_hbm, q_ref, k_ref, v_ref, out_ref,
    qbuf, kvbuf, kfeat, qfeat, vturn, obuf, reach_ref, valid_ref,
    send_sem, in_sem, fwd_sem, halo_sem, out_send_sem, out_sem, small_sem,
):
    frame = lax.axis_index("frame")
    me = lax.axis_index("head")
    half = frames // 2

    def swap(index, at):
        return lax.rem(index + jnp.where(at >= half, 4, 0), 8)

    group = swap(me, frame)
    has_prev = frame > 0
    has_next = frame < frames - 1
    prev_id = {"frame": frame - 1, "head": swap(group, frame - 1)}
    next_id = {"frame": frame + 1, "head": swap(group, frame + 1)}

    def peer(step):
        part = lax.rem(me // 4 + step // 4, 2) * 4 + lax.rem(me + step, 4)
        return part

    barrier = pltpu.get_barrier_semaphore()
    for step in range(1, 8):
        pl.semaphore_signal(
            barrier, inc=1, device_id={"frame": frame, "head": peer(step)}, device_id_type=MESH
        )

    @pl.when(has_prev)
    def _():
        pl.semaphore_signal(barrier, inc=1, device_id=prev_id, device_id_type=MESH)

    @pl.when(has_next)
    def _():
        pl.semaphore_signal(barrier, inc=1, device_id=next_id, device_id_type=MESH)

    pl.semaphore_wait(
        barrier, 7 + jnp.where(has_prev, 1, 0) + jnp.where(has_next, 1, 0)
    )

    def cols(of_group, head):
        return pl.ds(pl.multiple_of((of_group * LOCAL + head) * DH, DH), DH)

    order = (5, 1, 4, 3, 6, 2, 7)

    def send(at, head):
        ref = (q_ref, k_ref, v_ref)[at]
        land = qbuf.at[head, me] if at == 0 else kvbuf.at[at - 1, 1, head, me]
        for step in order:
            target = peer(step)
            pltpu.make_async_remote_copy(
                src_ref=ref.at[:, :, :, cols(swap(target, frame), head)],
                dst_ref=land,
                send_sem=send_sem.at[at],
                recv_sem=in_sem.at[at, head],
                device_id={"frame": frame, "head": target},
                device_id_type=MESH,
            ).start()
        pltpu.make_async_copy(
            ref.at[:, :, :, cols(group, head)], land, in_sem.at[at, head]
        ).start()

    for at, head in ((1, 0), (2, 0), (0, 0), (1, 1), (2, 1), (1, 2), (2, 2), (0, 1), (0, 2)):
        send(at, head)

    reach_copy = pltpu.make_async_copy(reach_hbm, reach_ref, small_sem.at[0])
    valid_copy = pltpu.make_async_copy(valid_hbm, valid_ref, small_sem.at[1])
    reach_copy.start()
    valid_copy.start()

    for part in range(8):
        for pair in range(PAIRS):
            kfeat[part, :, pair] = key_features(part, pair)

    vturn[:, DH:] = jnp.ones((3, 16, PAIRS * BLOCK), jnp.bfloat16)

    @pl.when(jnp.logical_not(has_prev))
    def _():
        kvbuf[:, 0] = jnp.zeros(kvbuf.shape[:1] + kvbuf.shape[2:], jnp.bfloat16)

    @pl.when(jnp.logical_not(has_next))
    def _():
        kvbuf[:, 2] = jnp.zeros(kvbuf.shape[:1] + kvbuf.shape[2:], jnp.bfloat16)

    def forward(head, kv, way):
        return pltpu.make_async_remote_copy(
            src_ref=kvbuf.at[kv, 1, head],
            dst_ref=kvbuf.at[kv, 2 - 2 * way, head],
            send_sem=fwd_sem.at[kv, way, head],
            recv_sem=halo_sem.at[kv, way, head],
            device_id=(prev_id, next_id)[way],
            device_id_type=MESH,
        )

    def pass_on(head):
        for kv in range(2):
            wait_bytes(kvbuf.at[kv, 1, head], in_sem.at[kv + 1, head])

            @pl.when(has_prev)
            def _():
                forward(head, kv, 0).start()

            @pl.when(has_next)
            def _():
                forward(head, kv, 1).start()

    reach_copy.wait()
    valid_copy.wait()
    live_own = valid_ref[0, frame]
    live_prev = jnp.where(has_prev, valid_ref[0, jnp.maximum(frame - 1, 0)], 0)
    live_next = jnp.where(has_next, valid_ref[0, jnp.minimum(frame + 1, frames - 1)], 0)

    def mask_rows(head, carry):
        row = group * LOCAL + head
        near = reach_ref[0, row] >= 1
        allowed = ((live_prev > 0) & near, live_own > 0, (live_next > 0) & near)
        for pair in range(PAIRS):
            base = query_features(pair, reach_ref[1, row], reach_ref[2, row])
            for slot in range(3):
                level = jnp.where(allowed[slot], jnp.float32(0.0), jnp.float32(-BIG))
                qfeat[head, pair, slot] = jnp.minimum(base, level).astype(jnp.bfloat16)
        return carry

    lax.fori_loop(0, LOCAL, mask_rows, 0)

    def turn_values(head):
        for slot in range(3):
            for pair in range(PAIRS):
                values = kvbuf[1, slot, head, :, :, pair].reshape(BLOCK, DH)
                vturn[slot, :DH, pair * BLOCK : (pair + 1) * BLOCK] = values.T

    def attend(head, pair):
        query = qbuf[head, :, :, pair].reshape(BLOCK, DH).T
        first, last = max(pair - 1, 0), min(pair + 2, PAIRS)
        scores = []
        for slot in range(3):
            stationary = jnp.concatenate([query, qfeat[head, pair, slot]], axis=0)
            for at in range(first, last):
                keys = kvbuf[0, slot, head, :, :, at].reshape(BLOCK, DH)
                tiles = kfeat[:, :, at].reshape(BLOCK, DH)
                scores.append(
                    jnp.dot(
                        jnp.concatenate([keys, tiles], axis=1),
                        stationary,
                        preferred_element_type=jnp.float32,
                    )
                )
        top = jnp.max(functools.reduce(jnp.maximum, scores), axis=0, keepdims=True)
        weights = jnp.concatenate(
            [jnp.exp2((s - top) * SCALE).astype(jnp.bfloat16) for s in scores], axis=0
        )
        turned = jnp.concatenate(
            [vturn[slot, :, first * BLOCK : last * BLOCK] for slot in range(3)], axis=1
        )
        mixed = jnp.dot(turned, weights, preferred_element_type=jnp.float32)
        result = mixed[:DH] / mixed[DH : DH + 1]
        result = jnp.where(live_own > 0, result, jnp.float32(0.0)).T.astype(jnp.bfloat16)
        obuf[head, :, :, pair] = result.reshape(8, ROWS, PIX, DH)

    def send_out(head, first, last):
        landing = out_ref.at[:, first:last, :, cols(group, head)]
        for step in order:
            target = peer(step)
            pltpu.make_async_remote_copy(
                src_ref=obuf.at[head, target, :, first:last],
                dst_ref=landing,
                send_sem=out_send_sem,
                recv_sem=out_sem,
                device_id={"frame": frame, "head": target},
                device_id_type=MESH,
            ).start()
        pltpu.make_async_copy(obuf.at[head, me, :, first:last], landing, out_sem).start()

    pass_on(0)

    def per_head(head, carry):
        @pl.when(head < LOCAL - 1)
        def _():
            pass_on(head + 1)

        wait_bytes(qbuf.at[head], in_sem.at[0, head])
        for kv in range(2):

            @pl.when(has_next)
            def _():
                forward(head, kv, 0).wait_recv()

            @pl.when(has_prev)
            def _():
                forward(head, kv, 1).wait_recv()

        turn_values(head)
        for first, last in ((0, 3), (3, PAIRS)):
            for pair in range(first, last):
                attend(head, pair)
            send_out(head, first, last)
        return carry

    lax.fori_loop(0, LOCAL, per_head, 0)

    for at in range(3):
        wait_bytes(qbuf.at[:, 0:7], send_sem.at[at])
    for head in range(LOCAL):
        for kv in range(2):

            @pl.when(has_prev)
            def _():
                forward(head, kv, 0).wait_send()

            @pl.when(has_next)
            def _():
                forward(head, kv, 1).wait_send()

    wait_bytes(obuf.at[:, 0:7], out_send_sem)
    wait_bytes(obuf, out_sem)


def solution(mesh):
    frames = mesh.shape["frame"]
    block = (8, ROWS, PAIRS, PIX, DH)

    def body(queries, keys, values, head_reach, frame_valid):
        grid = (ROWS, PAIRS, PIX, queries.shape[1])
        hbm = pl.BlockSpec(memory_space=pltpu.HBM)
        out = pl.pallas_call(
            functools.partial(kernel, frames),
            out_shape=pltpu.VMEM(grid, jnp.bfloat16),
            in_specs=[hbm] * 5,
            out_specs=pl.BlockSpec(memory_space=pltpu.VMEM),
            scratch_shapes=[
                pltpu.VMEM((LOCAL,) + block, jnp.bfloat16),
                pltpu.VMEM((2, 3, LOCAL) + block, jnp.bfloat16),
                pltpu.VMEM(block, jnp.bfloat16),
                pltpu.VMEM((LOCAL, PAIRS, 3, DH, BLOCK), jnp.bfloat16),
                pltpu.VMEM((3, DH + 16, PAIRS * BLOCK), jnp.bfloat16),
                pltpu.VMEM((LOCAL,) + block, jnp.bfloat16),
                pltpu.SMEM((3, head_reach.shape[0]), jnp.int32),
                pltpu.SMEM((1, frames), jnp.int32),
                pltpu.SemaphoreType.DMA((3,)),
                pltpu.SemaphoreType.DMA((3, LOCAL)),
                pltpu.SemaphoreType.DMA((2, 2, LOCAL)),
                pltpu.SemaphoreType.DMA((2, 2, LOCAL)),
                pltpu.SemaphoreType.DMA,
                pltpu.SemaphoreType.DMA,
                pltpu.SemaphoreType.DMA((2,)),
            ],
            compiler_params=pltpu.CompilerParams(
                collective_id=0, has_side_effects=True, vmem_limit_bytes=VMEM
            ),
        )(
            head_reach.T,
            frame_valid.reshape(1, frames),
            *(
                pltpu.with_memory_space_constraint(array.reshape(grid), pltpu.HBM)
                for array in (queries, keys, values)
            ),
        )
        return out.reshape(queries.shape)

    rows = P(("frame", "head"), None)
    return jax.shard_map(
        body, mesh=mesh, in_specs=(rows, rows, rows, P(), P()), out_specs=rows, check_vma=False
    )
```

```python
import functools
import math

import jax
import jax.numpy as jnp
from jax import lax
from jax.experimental import pallas as pl
from jax.experimental.pallas import tpu as pltpu
from jax.sharding import PartitionSpec as P

DH = 128
ROWS = 2
PAIRS = 5
PIX = 16
TW = 10
LOCAL = 3
VMEM = 62 * 2**20
MESH = pl.DeviceIdType.MESH
BIG = float(2**20)
SCALE = math.log2(math.e) / math.sqrt(DH)


def query_features(pair, reach_h, reach_w):
    shape = (8 * ROWS * PIX, DH)
    row = lax.broadcasted_iota(jnp.int32, shape, 0)
    col = lax.broadcasted_iota(jnp.int32, shape, 1)
    tile_y = row >> 7
    tile_x = 2 * pair + ((row & 15) >> 3)
    key_y = (col >= TW).astype(jnp.int32)
    key_x = col - TW * key_y
    size_y = jnp.minimum(2 * reach_h + 1, 2)
    size_x = jnp.minimum(2 * reach_w + 1, TW)
    low_y = jnp.clip(tile_y - reach_h, 0, 2 - size_y)
    low_x = jnp.clip(tile_x - reach_w, 0, TW - size_x)
    inside = (key_y >= low_y) & (key_y < low_y + size_y)
    inside = inside & (key_x >= low_x) & (key_x < low_x + size_x)
    return jnp.where(inside, jnp.float32(0.0), jnp.float32(-BIG))


def key_features(part, pair):
    shape = (ROWS, PIX, DH)
    pix = lax.broadcasted_iota(jnp.int32, shape, 1)
    col = lax.broadcasted_iota(jnp.int32, shape, 2)
    tile = (part // 4) * TW + 2 * pair + (pix >> 3)
    return jnp.where(col == tile, jnp.float32(1.0), jnp.float32(0.0)).astype(jnp.bfloat16)


def wait_bytes(ref, sem):
    pltpu.make_async_copy(ref, ref, sem).wait()


def kernel(
    frames, reach_hbm, valid_hbm, q_ref, k_ref, v_ref, out_ref,
    qbuf, kvbuf, kfeat, obuf, reach_ref, valid_ref,
    send_sem, in_sem, fwd_sem, halo_sem, out_send_sem, out_sem, small_sem,
):
    frame = lax.axis_index("frame")
    me = lax.axis_index("head")
    half = frames // 2

    def swap(index, at):
        return lax.rem(index + jnp.where(at >= half, 4, 0), 8)

    group = swap(me, frame)
    odd = lax.rem(frame, 2)
    way = 2 * odd - 1
    z_slot, mate_slot = 2 * odd, 2 - 2 * odd
    has_z = (frame + way >= 0) & (frame + way < frames)
    has_relay = (frame - 2 * way >= 0) & (frame - 2 * way < frames)

    def device(at):
        return {"frame": at, "head": swap(group, at)}

    mate_id = device(frame - way)
    z_id = device(frame + way)
    z_far_id = device(frame + 2 * way)
    relay_id = device(frame - 2 * way)

    def peer(step):
        part = lax.rem(me // 4 + step // 4, 2) * 4 + lax.rem(me + step, 4)
        return part

    barrier = pltpu.get_barrier_semaphore()
    for step in range(1, 8):
        pl.semaphore_signal(
            barrier, inc=1, device_id={"frame": frame, "head": peer(step)}, device_id_type=MESH
        )

    pl.semaphore_signal(barrier, inc=1, device_id=mate_id, device_id_type=MESH)

    @pl.when(has_z)
    def _():
        pl.semaphore_signal(barrier, inc=1, device_id=z_id, device_id_type=MESH)
        pl.semaphore_signal(barrier, inc=1, device_id=z_far_id, device_id_type=MESH)

    @pl.when(has_relay)
    def _():
        pl.semaphore_signal(barrier, inc=1, device_id=relay_id, device_id_type=MESH)

    pl.semaphore_wait(
        barrier, 8 + jnp.where(has_z, 2, 0) + jnp.where(has_relay, 1, 0)
    )

    def cols(of_group, head):
        return pl.ds(pl.multiple_of((of_group * LOCAL + head) * DH, DH), DH)

    order = (5, 1, 4, 3, 6, 2, 7)

    def send(at, head):
        ref = (q_ref, k_ref, v_ref)[at]
        land = qbuf.at[head, me] if at == 0 else kvbuf.at[at - 1, 1, head, me]
        for step in order:
            target = peer(step)
            pltpu.make_async_remote_copy(
                src_ref=ref.at[:, :, :, cols(swap(target, frame), head)],
                dst_ref=land,
                send_sem=send_sem.at[at],
                recv_sem=in_sem.at[at, head],
                device_id={"frame": frame, "head": target},
                device_id_type=MESH,
            ).start()
        pltpu.make_async_copy(
            ref.at[:, :, :, cols(group, head)], land, in_sem.at[at, head]
        ).start()

    for at, head in ((1, 0), (2, 0), (0, 0), (1, 1), (2, 1), (1, 2), (2, 2), (0, 1), (0, 2)):
        send(at, head)

    reach_copy = pltpu.make_async_copy(reach_hbm, reach_ref, small_sem.at[0])
    valid_copy = pltpu.make_async_copy(valid_hbm, valid_ref, small_sem.at[1])
    reach_copy.start()
    valid_copy.start()

    for part in range(8):
        for pair in range(PAIRS):
            kfeat[part, :, pair] = key_features(part, pair)

    @pl.when(jnp.logical_not(has_z))
    def _():
        kvbuf[:, z_slot] = jnp.zeros(kvbuf.shape[:1] + kvbuf.shape[2:], jnp.bfloat16)

    def forward(head, kv, side, from_slot, to_slot, target):
        return pltpu.make_async_remote_copy(
            src_ref=kvbuf.at[kv, from_slot, head],
            dst_ref=kvbuf.at[kv, to_slot, head],
            send_sem=fwd_sem.at[kv, side, head],
            recv_sem=halo_sem.at[kv, side, head],
            device_id=target,
            device_id_type=MESH,
        )

    def to_mate(head, kv):
        return forward(head, kv, 0, 1, z_slot, mate_id)

    def values_to_z(head):
        return forward(head, 1, 1, 1, mate_slot, z_id)

    def relay_keys(head):
        return forward(head, 0, 1, mate_slot, z_slot, relay_id)

    def pass_on(head):
        wait_bytes(kvbuf.at[0, 1, head], in_sem.at[1, head])
        to_mate(head, 0).start()
        wait_bytes(kvbuf.at[1, 1, head], in_sem.at[2, head])

        @pl.when(has_z)
        def _():
            values_to_z(head).start()

        to_mate(head, 1).start()
        to_mate(head, 0).wait_recv()

        @pl.when(has_relay)
        def _():
            relay_keys(head).start()

    reach_copy.wait()
    valid_copy.wait()
    live_own = valid_ref[0, frame]
    live_prev = jnp.where(frame > 0, valid_ref[0, jnp.maximum(frame - 1, 0)], 0)
    live_next = jnp.where(
        frame < frames - 1, valid_ref[0, jnp.minimum(frame + 1, frames - 1)], 0
    )

    def attend(head, pair):
        row = group * LOCAL + head
        reach_t = reach_ref[0, row]
        base = query_features(pair, reach_ref[1, row], reach_ref[2, row])
        near = reach_t >= 1
        allowed = ((live_prev > 0) & near, live_own > 0, (live_next > 0) & near)
        query = qbuf[head, :, :, pair].reshape(8 * ROWS * PIX, DH)
        first, last = max(pair - 1, 0), min(pair + 2, PAIRS)
        count = 8 * ROWS * (last - first) * PIX
        tiles = kfeat[:, :, first:last].reshape(count, DH)
        scores = []
        for slot in range(3):
            features = jnp.minimum(
                base, jnp.where(allowed[slot], jnp.float32(0.0), jnp.float32(-BIG))
            ).astype(jnp.bfloat16)
            keys = kvbuf[0, slot, head, :, :, first:last].reshape(count, DH)
            scores.append(
                lax.dot_general(
                    jnp.concatenate([query, features], axis=1),
                    jnp.concatenate([keys, tiles], axis=1),
                    (((1,), (1,)), ((), ())),
                    preferred_element_type=jnp.float32,
                )
            )
        top = functools.reduce(jnp.maximum, [jnp.max(s, axis=1, keepdims=True) for s in scores])
        ones = jnp.ones((count, DH), jnp.bfloat16)
        mixed = None
        for slot in range(3):
            weights = jnp.exp2((scores[slot] - top) * SCALE).astype(jnp.bfloat16)
            values = kvbuf[1, slot, head, :, :, first:last].reshape(count, DH)
            term = jnp.dot(
                weights,
                jnp.concatenate([values, ones], axis=1),
                preferred_element_type=jnp.float32,
            )
            mixed = term if mixed is None else mixed + term
        result = mixed[:, :DH] / mixed[:, DH:]
        result = jnp.where(live_own > 0, result, jnp.float32(0.0)).astype(jnp.bfloat16)
        obuf[head, :, :, pair] = result.reshape(8, ROWS, PIX, DH)

    def send_out(head, first, last):
        landing = out_ref.at[:, first:last, :, cols(group, head)]
        for step in order:
            target = peer(step)
            pltpu.make_async_remote_copy(
                src_ref=obuf.at[head, target, :, first:last],
                dst_ref=landing,
                send_sem=out_send_sem,
                recv_sem=out_sem,
                device_id={"frame": frame, "head": target},
                device_id_type=MESH,
            ).start()
        pltpu.make_async_copy(obuf.at[head, me, :, first:last], landing, out_sem).start()

    pass_on(0)

    def per_head(head, carry):
        @pl.when(head < LOCAL - 1)
        def _():
            pass_on(head + 1)

        wait_bytes(qbuf.at[head], in_sem.at[0, head])
        to_mate(head, 1).wait_recv()

        @pl.when(has_z)
        def _():
            relay_keys(head).wait_recv()
            values_to_z(head).wait_recv()

        for first, last in ((0, 3), (3, PAIRS)):
            for pair in range(first, last):
                attend(head, pair)
            send_out(head, first, last)
        return carry

    lax.fori_loop(0, LOCAL, per_head, 0)

    for at in range(3):
        wait_bytes(qbuf.at[:, 0:7], send_sem.at[at])
    for head in range(LOCAL):
        to_mate(head, 0).wait_send()
        to_mate(head, 1).wait_send()

        @pl.when(has_z)
        def _():
            values_to_z(head).wait_send()

        @pl.when(has_relay)
        def _():
            relay_keys(head).wait_send()

    wait_bytes(obuf.at[:, 0:7], out_send_sem)
    wait_bytes(obuf, out_sem)


def solution(mesh):
    frames = mesh.shape["frame"]
    block = (8, ROWS, PAIRS, PIX, DH)

    def body(queries, keys, values, head_reach, frame_valid):
        grid = (ROWS, PAIRS, PIX, queries.shape[1])
        hbm = pl.BlockSpec(memory_space=pltpu.HBM)
        out = pl.pallas_call(
            functools.partial(kernel, frames),
            out_shape=pltpu.VMEM(grid, jnp.bfloat16),
            in_specs=[hbm] * 5,
            out_specs=pl.BlockSpec(memory_space=pltpu.VMEM),
            scratch_shapes=[
                pltpu.VMEM((LOCAL,) + block, jnp.bfloat16),
                pltpu.VMEM((2, 3, LOCAL) + block, jnp.bfloat16),
                pltpu.VMEM(block, jnp.bfloat16),
                pltpu.VMEM((LOCAL,) + block, jnp.bfloat16),
                pltpu.SMEM((3, head_reach.shape[0]), jnp.int32),
                pltpu.SMEM((1, frames), jnp.int32),
                pltpu.SemaphoreType.DMA((3,)),
                pltpu.SemaphoreType.DMA((3, LOCAL)),
                pltpu.SemaphoreType.DMA((2, 2, LOCAL)),
                pltpu.SemaphoreType.DMA((2, 2, LOCAL)),
                pltpu.SemaphoreType.DMA,
                pltpu.SemaphoreType.DMA,
                pltpu.SemaphoreType.DMA((2,)),
            ],
            compiler_params=pltpu.CompilerParams(
                collective_id=0, has_side_effects=True, vmem_limit_bytes=VMEM
            ),
        )(
            head_reach.T,
            frame_valid.reshape(1, frames),
            *(
                pltpu.with_memory_space_constraint(array.reshape(grid), pltpu.HBM)
                for array in (queries, keys, values)
            ),
        )
        return out.reshape(queries.shape)

    rows = P(("frame", "head"), None)
    return jax.shard_map(
        body, mesh=mesh, in_specs=(rows, rows, rows, P(), P()), out_specs=rows, check_vma=False
    )
```

```python
import functools
import math

import jax
import jax.numpy as jnp
from jax import lax
from jax.experimental import pallas as pl
from jax.experimental.pallas import tpu as pltpu
from jax.sharding import PartitionSpec as P

DH = 128
ROWS = 2
PAIRS = 5
PIX = 16
TW = 10
LOCAL = 3
VMEM = 62 * 2**20
MESH = pl.DeviceIdType.MESH
BIG = float(2**20)
SCALE = math.log2(math.e) / math.sqrt(DH)


def query_features(pair, reach_h, reach_w):
    shape = (8 * ROWS * PIX, DH)
    row = lax.broadcasted_iota(jnp.int32, shape, 0)
    col = lax.broadcasted_iota(jnp.int32, shape, 1)
    tile_y = row >> 7
    tile_x = 2 * pair + ((row & 15) >> 3)
    key_y = (col >= TW).astype(jnp.int32)
    key_x = col - TW * key_y
    size_y = jnp.minimum(2 * reach_h + 1, 2)
    size_x = jnp.minimum(2 * reach_w + 1, TW)
    low_y = jnp.clip(tile_y - reach_h, 0, 2 - size_y)
    low_x = jnp.clip(tile_x - reach_w, 0, TW - size_x)
    inside = (key_y >= low_y) & (key_y < low_y + size_y)
    inside = inside & (key_x >= low_x) & (key_x < low_x + size_x)
    return jnp.where(inside, jnp.float32(0.0), jnp.float32(-BIG))


def key_features(part, pair):
    shape = (ROWS, PIX, DH)
    pix = lax.broadcasted_iota(jnp.int32, shape, 1)
    col = lax.broadcasted_iota(jnp.int32, shape, 2)
    tile = (part // 4) * TW + 2 * pair + (pix >> 3)
    return jnp.where(col == tile, jnp.float32(1.0), jnp.float32(0.0)).astype(jnp.bfloat16)


def wait_bytes(ref, sem):
    pltpu.make_async_copy(ref, ref, sem).wait()


def kernel(
    frames, reach_hbm, valid_hbm, q_ref, k_ref, v_ref, out_ref,
    qbuf, kvbuf, kfeat, obuf, reach_ref, valid_ref,
    send_sem, in_sem, fwd_sem, halo_sem, out_send_sem, out_sem, small_sem, ready_sem,
):
    frame = lax.axis_index("frame")
    me = lax.axis_index("head")
    half = frames // 2

    def swap(index, at):
        return lax.rem(index + jnp.where(at >= half, 4, 0), 8)

    group = swap(me, frame)
    odd = lax.rem(frame, 2)
    way = 2 * odd - 1
    z_slot, mate_slot = 2 * odd, 2 - 2 * odd
    has_z = (frame + way >= 0) & (frame + way < frames)
    has_relay = (frame - 2 * way >= 0) & (frame - 2 * way < frames)

    def device(at):
        return {"frame": at, "head": swap(group, at)}

    mate_id = device(frame - way)
    z_id = device(frame + way)
    z_far_id = device(frame + 2 * way)
    relay_id = device(frame - 2 * way)

    def peer(step):
        part = lax.rem(me // 4 + step // 4, 2) * 4 + lax.rem(me + step, 4)
        return part

    barrier = pltpu.get_barrier_semaphore()
    for step in range(1, 8):
        pl.semaphore_signal(
            barrier, inc=1, device_id={"frame": frame, "head": peer(step)}, device_id_type=MESH
        )

    pl.semaphore_signal(barrier, inc=1, device_id=mate_id, device_id_type=MESH)

    even = odd == 0

    @pl.when(even & has_z)
    def _():
        pl.semaphore_signal(barrier, inc=1, device_id=z_id, device_id_type=MESH)
        pl.semaphore_signal(barrier, inc=1, device_id=z_far_id, device_id_type=MESH)

    @pl.when((odd == 1) & has_relay)
    def _():
        pl.semaphore_signal(barrier, inc=1, device_id=relay_id, device_id_type=MESH)

    greeted = jnp.where(even, jnp.where(has_relay, 1, 0), jnp.where(has_z, 2, 0))
    pl.semaphore_wait(barrier, 8 + greeted)

    @pl.when((odd == 1) & has_z)
    def _():
        pl.semaphore_signal(ready_sem, inc=1, device_id=z_id, device_id_type=MESH)
        pl.semaphore_signal(ready_sem, inc=1, device_id=z_far_id, device_id_type=MESH)

    def cols(of_group, head):
        return pl.ds(pl.multiple_of((of_group * LOCAL + head) * DH, DH), DH)

    order = (5, 1, 4, 3, 6, 2, 7)

    def send(at, head):
        ref = (q_ref, k_ref, v_ref)[at]
        land = qbuf.at[head, me] if at == 0 else kvbuf.at[at - 1, 1, head, me]
        for step in order:
            target = peer(step)
            pltpu.make_async_remote_copy(
                src_ref=ref.at[:, :, :, cols(swap(target, frame), head)],
                dst_ref=land,
                send_sem=send_sem.at[at],
                recv_sem=in_sem.at[at, head],
                device_id={"frame": frame, "head": target},
                device_id_type=MESH,
            ).start()
        pltpu.make_async_copy(
            ref.at[:, :, :, cols(group, head)], land, in_sem.at[at, head]
        ).start()

    for at, head in ((1, 0), (2, 0), (0, 0), (1, 1), (2, 1), (1, 2), (2, 2), (0, 1), (0, 2)):
        send(at, head)

    reach_copy = pltpu.make_async_copy(reach_hbm, reach_ref, small_sem.at[0])
    valid_copy = pltpu.make_async_copy(valid_hbm, valid_ref, small_sem.at[1])
    reach_copy.start()
    valid_copy.start()

    for part in range(8):
        for pair in range(PAIRS):
            kfeat[part, :, pair] = key_features(part, pair)

    @pl.when(jnp.logical_not(has_z))
    def _():
        kvbuf[:, z_slot] = jnp.zeros(kvbuf.shape[:1] + kvbuf.shape[2:], jnp.bfloat16)

    def forward(head, kv, side, from_slot, to_slot, target):
        return pltpu.make_async_remote_copy(
            src_ref=kvbuf.at[kv, from_slot, head],
            dst_ref=kvbuf.at[kv, to_slot, head],
            send_sem=fwd_sem.at[kv, side, head],
            recv_sem=halo_sem.at[kv, side, head],
            device_id=target,
            device_id_type=MESH,
        )

    def to_mate(head, kv):
        return forward(head, kv, 0, 1, z_slot, mate_id)

    def values_to_z(head):
        return forward(head, 1, 1, 1, mate_slot, z_id)

    def relay_keys(head):
        return forward(head, 0, 1, mate_slot, z_slot, relay_id)

    def pass_on(head):
        wait_bytes(kvbuf.at[0, 1, head], in_sem.at[1, head])
        to_mate(head, 0).start()
        wait_bytes(kvbuf.at[1, 1, head], in_sem.at[2, head])

        @pl.when(has_z)
        def _():
            values_to_z(head).start()

        to_mate(head, 1).start()
        to_mate(head, 0).wait_recv()

        @pl.when(has_relay)
        def _():
            relay_keys(head).start()

    reach_copy.wait()
    valid_copy.wait()
    live_own = valid_ref[0, frame]
    live_prev = jnp.where(frame > 0, valid_ref[0, jnp.maximum(frame - 1, 0)], 0)
    live_next = jnp.where(
        frame < frames - 1, valid_ref[0, jnp.minimum(frame + 1, frames - 1)], 0
    )

    def attend(head, pair):
        row = group * LOCAL + head
        reach_t = reach_ref[0, row]
        base = query_features(pair, reach_ref[1, row], reach_ref[2, row])
        near = reach_t >= 1
        allowed = ((live_prev > 0) & near, live_own > 0, (live_next > 0) & near)
        query = qbuf[head, :, :, pair].reshape(8 * ROWS * PIX, DH)
        first, last = max(pair - 1, 0), min(pair + 2, PAIRS)
        count = 8 * ROWS * (last - first) * PIX
        tiles = kfeat[:, :, first:last].reshape(count, DH)
        scores = []
        for slot in range(3):
            features = jnp.minimum(
                base, jnp.where(allowed[slot], jnp.float32(0.0), jnp.float32(-BIG))
            ).astype(jnp.bfloat16)
            keys = kvbuf[0, slot, head, :, :, first:last].reshape(count, DH)
            scores.append(
                lax.dot_general(
                    jnp.concatenate([query, features], axis=1),
                    jnp.concatenate([keys, tiles], axis=1),
                    (((1,), (1,)), ((), ())),
                    preferred_element_type=jnp.float32,
                )
            )
        top = functools.reduce(jnp.maximum, [jnp.max(s, axis=1, keepdims=True) for s in scores])
        ones = jnp.ones((count, DH), jnp.bfloat16)
        mixed = None
        for slot in range(3):
            weights = jnp.exp2((scores[slot] - top) * SCALE).astype(jnp.bfloat16)
            values = kvbuf[1, slot, head, :, :, first:last].reshape(count, DH)
            term = jnp.dot(
                weights,
                jnp.concatenate([values, ones], axis=1),
                preferred_element_type=jnp.float32,
            )
            mixed = term if mixed is None else mixed + term
        result = mixed[:, :DH] / mixed[:, DH:]
        result = jnp.where(live_own > 0, result, jnp.float32(0.0)).astype(jnp.bfloat16)
        obuf[head, :, :, pair] = result.reshape(8, ROWS, PIX, DH)

    def send_out(head, first, last):
        landing = out_ref.at[:, first:last, :, cols(group, head)]
        for step in order:
            target = peer(step)
            pltpu.make_async_remote_copy(
                src_ref=obuf.at[head, target, :, first:last],
                dst_ref=landing,
                send_sem=out_send_sem,
                recv_sem=out_sem,
                device_id={"frame": frame, "head": target},
                device_id_type=MESH,
            ).start()
        pltpu.make_async_copy(obuf.at[head, me, :, first:last], landing, out_sem).start()

    @pl.when(jnp.where(even, has_z, has_relay))
    def _():
        pl.semaphore_wait(ready_sem, 1)

    pass_on(0)

    def per_head(head, carry):
        @pl.when(head < LOCAL - 1)
        def _():
            pass_on(head + 1)

        wait_bytes(qbuf.at[head], in_sem.at[0, head])
        last_head = head == LOCAL - 1

        @pl.when(last_head)
        def _():
            for done in range(LOCAL - 1):
                send_out(done, 0, PAIRS)

        to_mate(head, 1).wait_recv()

        @pl.when(has_z)
        def _():
            relay_keys(head).wait_recv()
            values_to_z(head).wait_recv()

        for first, last in ((0, 2), (2, 4), (4, PAIRS)):
            for pair in range(first, last):
                attend(head, pair)

            @pl.when(last_head)
            def _():
                send_out(head, first, last)

        return carry

    lax.fori_loop(0, LOCAL, per_head, 0)

    for at in range(3):
        wait_bytes(qbuf.at[:, 0:7], send_sem.at[at])
    for head in range(LOCAL):
        to_mate(head, 0).wait_send()
        to_mate(head, 1).wait_send()

        @pl.when(has_z)
        def _():
            values_to_z(head).wait_send()

        @pl.when(has_relay)
        def _():
            relay_keys(head).wait_send()

    wait_bytes(obuf.at[:, 0:7], out_send_sem)
    wait_bytes(obuf, out_sem)


def solution(mesh):
    frames = mesh.shape["frame"]
    block = (8, ROWS, PAIRS, PIX, DH)

    def body(queries, keys, values, head_reach, frame_valid):
        grid = (ROWS, PAIRS, PIX, queries.shape[1])
        hbm = pl.BlockSpec(memory_space=pltpu.HBM)
        out = pl.pallas_call(
            functools.partial(kernel, frames),
            out_shape=pltpu.VMEM(grid, jnp.bfloat16),
            in_specs=[hbm] * 5,
            out_specs=pl.BlockSpec(memory_space=pltpu.VMEM),
            scratch_shapes=[
                pltpu.VMEM((LOCAL,) + block, jnp.bfloat16),
                pltpu.VMEM((2, 3, LOCAL) + block, jnp.bfloat16),
                pltpu.VMEM(block, jnp.bfloat16),
                pltpu.VMEM((LOCAL,) + block, jnp.bfloat16),
                pltpu.SMEM((3, head_reach.shape[0]), jnp.int32),
                pltpu.SMEM((1, frames), jnp.int32),
                pltpu.SemaphoreType.DMA((3,)),
                pltpu.SemaphoreType.DMA((3, LOCAL)),
                pltpu.SemaphoreType.DMA((2, 2, LOCAL)),
                pltpu.SemaphoreType.DMA((2, 2, LOCAL)),
                pltpu.SemaphoreType.DMA,
                pltpu.SemaphoreType.DMA,
                pltpu.SemaphoreType.DMA((2,)),
                pltpu.SemaphoreType.REGULAR,
            ],
            compiler_params=pltpu.CompilerParams(
                collective_id=0, has_side_effects=True, vmem_limit_bytes=VMEM
            ),
        )(
            head_reach.T,
            frame_valid.reshape(1, frames),
            *(
                pltpu.with_memory_space_constraint(array.reshape(grid), pltpu.HBM)
                for array in (queries, keys, values)
            ),
        )
        return out.reshape(queries.shape)

    rows = P(("frame", "head"), None)
    return jax.shard_map(
        body, mesh=mesh, in_specs=(rows, rows, rows, P(), P()), out_specs=rows, check_vma=False
    )
```

```python
import functools
import math

import jax
import jax.numpy as jnp
from jax import lax
from jax.experimental import pallas as pl
from jax.experimental.pallas import tpu as pltpu
from jax.sharding import PartitionSpec as P

DH = 128
ROWS = 2
PAIRS = 5
PIX = 16
TW = 10
LOCAL = 3
VMEM = 62 * 2**20
MESH = pl.DeviceIdType.MESH
BIG = float(2**20)
SCALE = math.log2(math.e) / math.sqrt(DH)


def query_features(pair, reach_h, reach_w):
    shape = (8 * ROWS * PIX, DH)
    row = lax.broadcasted_iota(jnp.int32, shape, 0)
    col = lax.broadcasted_iota(jnp.int32, shape, 1)
    tile_y = row >> 7
    tile_x = 2 * pair + ((row & 15) >> 3)
    key_y = (col >= TW).astype(jnp.int32)
    key_x = col - TW * key_y
    size_y = jnp.minimum(2 * reach_h + 1, 2)
    size_x = jnp.minimum(2 * reach_w + 1, TW)
    low_y = jnp.clip(tile_y - reach_h, 0, 2 - size_y)
    low_x = jnp.clip(tile_x - reach_w, 0, TW - size_x)
    inside = (key_y >= low_y) & (key_y < low_y + size_y)
    inside = inside & (key_x >= low_x) & (key_x < low_x + size_x)
    return jnp.where(inside, jnp.float32(0.0), jnp.float32(-BIG))


def key_features(part, pair):
    shape = (ROWS, PIX, DH)
    pix = lax.broadcasted_iota(jnp.int32, shape, 1)
    col = lax.broadcasted_iota(jnp.int32, shape, 2)
    tile = (part // 4) * TW + 2 * pair + (pix >> 3)
    return jnp.where(col == tile, jnp.float32(1.0), jnp.float32(0.0)).astype(jnp.bfloat16)


def wait_bytes(ref, sem):
    pltpu.make_async_copy(ref, ref, sem).wait()


def kernel(
    frames, reach_hbm, valid_hbm, q_ref, k_ref, v_ref, out_ref,
    qbuf, kvbuf, kfeat, obuf, reach_ref, valid_ref,
    send_sem, in_sem, fwd_sem, halo_sem, out_send_sem, out_sem, small_sem, ready_sem,
):
    frame = lax.axis_index("frame")
    me = lax.axis_index("head")
    half = frames // 2

    def swap(index, at):
        return lax.rem(index + jnp.where(at >= half, 4, 0), 8)

    group = swap(me, frame)
    has_prev = frame > 0
    has_next = frame < frames - 1
    prev_id = {"frame": frame - 1, "head": swap(group, frame - 1)}
    next_id = {"frame": frame + 1, "head": swap(group, frame + 1)}

    def peer(step):
        part = lax.rem(me // 4 + step // 4, 2) * 4 + lax.rem(me + step, 4)
        return part

    barrier = pltpu.get_barrier_semaphore()
    for step in range(1, 8):
        pl.semaphore_signal(
            barrier, inc=1, device_id={"frame": frame, "head": peer(step)}, device_id_type=MESH
        )

    even = lax.rem(frame, 2) == 0
    odd = jnp.logical_not(even)

    def greet(sem, target):
        pl.semaphore_signal(sem, inc=1, device_id=target, device_id_type=MESH)

    @pl.when(has_prev)
    def _():
        greet(barrier, prev_id)

    @pl.when(even)
    def _():
        greet(barrier, next_id)

    pl.semaphore_wait(barrier, 8 + jnp.where(odd & has_next, 1, 0))

    @pl.when(odd & has_next)
    def _():
        greet(ready_sem, next_id)

    def cols(of_group, head):
        return pl.ds(pl.multiple_of((of_group * LOCAL + head) * DH, DH), DH)

    order = (5, 1, 4, 3, 6, 2, 7)

    def send(at, head):
        ref = (q_ref, k_ref, v_ref)[at]
        land = qbuf.at[head, me] if at == 0 else kvbuf.at[at - 1, 1, head, me]
        for step in order:
            target = peer(step)
            pltpu.make_async_remote_copy(
                src_ref=ref.at[:, :, :, cols(swap(target, frame), head)],
                dst_ref=land,
                send_sem=send_sem.at[at],
                recv_sem=in_sem.at[at, head],
                device_id={"frame": frame, "head": target},
                device_id_type=MESH,
            ).start()
        pltpu.make_async_copy(
            ref.at[:, :, :, cols(group, head)], land, in_sem.at[at, head]
        ).start()

    for at, head in ((1, 0), (2, 0), (0, 0), (1, 1), (2, 1), (1, 2), (2, 2), (0, 1), (0, 2)):
        send(at, head)

    reach_copy = pltpu.make_async_copy(reach_hbm, reach_ref, small_sem.at[0])
    valid_copy = pltpu.make_async_copy(valid_hbm, valid_ref, small_sem.at[1])
    reach_copy.start()
    valid_copy.start()

    for part in range(8):
        for pair in range(PAIRS):
            kfeat[part, :, pair] = key_features(part, pair)

    @pl.when(jnp.logical_not(has_prev))
    def _():
        kvbuf[:, 0] = jnp.zeros(kvbuf.shape[:1] + kvbuf.shape[2:], jnp.bfloat16)

    @pl.when(jnp.logical_not(has_next))
    def _():
        kvbuf[:, 2] = jnp.zeros(kvbuf.shape[:1] + kvbuf.shape[2:], jnp.bfloat16)

    def forward(head, kv, way):
        return pltpu.make_async_remote_copy(
            src_ref=kvbuf.at[kv, 1, head],
            dst_ref=kvbuf.at[kv, 2 - 2 * way, head],
            send_sem=fwd_sem.at[kv, way, head],
            recv_sem=halo_sem.at[kv, way, head],
            device_id=(prev_id, next_id)[way],
            device_id_type=MESH,
        )

    def pass_on(head):
        for kv in range(2):
            wait_bytes(kvbuf.at[kv, 1, head], in_sem.at[kv + 1, head])

            @pl.when(has_prev)
            def _():
                forward(head, kv, 0).start()

            @pl.when(has_next)
            def _():
                forward(head, kv, 1).start()

    reach_copy.wait()
    valid_copy.wait()
    live_own = valid_ref[0, frame]
    live_prev = jnp.where(has_prev, valid_ref[0, jnp.maximum(frame - 1, 0)], 0)
    live_next = jnp.where(has_next, valid_ref[0, jnp.minimum(frame + 1, frames - 1)], 0)

    def attend(head, pair):
        row = group * LOCAL + head
        reach_t = reach_ref[0, row]
        base = query_features(pair, reach_ref[1, row], reach_ref[2, row])
        near = reach_t >= 1
        allowed = ((live_prev > 0) & near, live_own > 0, (live_next > 0) & near)
        query = qbuf[head, :, :, pair].reshape(8 * ROWS * PIX, DH)
        near_pairs = pl.ds(jnp.clip(pair - 1, 0, PAIRS - 3), 3)
        count = 8 * ROWS * 3 * PIX
        tiles = kfeat[:, :, near_pairs].reshape(count, DH)
        scores = []
        for slot in range(3):
            features = jnp.minimum(
                base, jnp.where(allowed[slot], jnp.float32(0.0), jnp.float32(-BIG))
            ).astype(jnp.bfloat16)
            keys = kvbuf[0, slot, head, :, :, near_pairs].reshape(count, DH)
            scores.append(
                lax.dot_general(
                    jnp.concatenate([query, features], axis=1),
                    jnp.concatenate([keys, tiles], axis=1),
                    (((1,), (1,)), ((), ())),
                    preferred_element_type=jnp.float32,
                )
            )
        top = jnp.max(functools.reduce(jnp.maximum, scores), axis=1, keepdims=True)
        ones = jnp.ones((count, DH), jnp.bfloat16)
        mixed = None
        for slot in range(3):
            weights = jnp.exp2((scores[slot] - top) * SCALE).astype(jnp.bfloat16)
            values = kvbuf[1, slot, head, :, :, near_pairs].reshape(count, DH)
            term = jnp.dot(
                weights,
                jnp.concatenate([values, ones], axis=1),
                preferred_element_type=jnp.float32,
            )
            mixed = term if mixed is None else mixed + term
        result = mixed[:, :DH] / mixed[:, DH:]
        result = jnp.where(live_own > 0, result, jnp.float32(0.0)).astype(jnp.bfloat16)
        obuf[head, :, :, pair] = result.reshape(8, ROWS, PIX, DH)

    def send_out(head, first, last):
        landing = out_ref.at[:, first:last, :, cols(group, head)]
        for step in order:
            target = peer(step)
            pltpu.make_async_remote_copy(
                src_ref=obuf.at[head, target, :, first:last],
                dst_ref=landing,
                send_sem=out_send_sem,
                recv_sem=out_sem,
                device_id={"frame": frame, "head": target},
                device_id_type=MESH,
            ).start()
        pltpu.make_async_copy(obuf.at[head, me, :, first:last], landing, out_sem).start()

    @pl.when(even & has_prev)
    def _():
        pl.semaphore_wait(ready_sem, 1)

    pass_on(0)

    def per_head(head, carry):
        @pl.when(head < LOCAL - 1)
        def _():
            pass_on(head + 1)

        wait_bytes(qbuf.at[head], in_sem.at[0, head])
        for kv in range(2):

            @pl.when(has_next)
            def _():
                forward(head, kv, 0).wait_recv()

            @pl.when(has_prev)
            def _():
                forward(head, kv, 1).wait_recv()

        def per_pair(pair, carry):
            attend(head, pair)
            for first, last in ((0, 3), (3, PAIRS)):

                @pl.when(pair == last - 1)
                def _():
                    send_out(head, first, last)

            return carry

        lax.fori_loop(0, PAIRS, per_pair, 0)
        return carry

    lax.fori_loop(0, LOCAL, per_head, 0)

    for at in range(3):
        wait_bytes(qbuf.at[:, 0:7], send_sem.at[at])
    for head in range(LOCAL):
        for kv in range(2):

            @pl.when(has_prev)
            def _():
                forward(head, kv, 0).wait_send()

            @pl.when(has_next)
            def _():
                forward(head, kv, 1).wait_send()

    wait_bytes(obuf.at[:, 0:7], out_send_sem)
    wait_bytes(obuf, out_sem)


def solution(mesh):
    frames = mesh.shape["frame"]
    block = (8, ROWS, PAIRS, PIX, DH)

    def body(queries, keys, values, head_reach, frame_valid):
        grid = (ROWS, PAIRS, PIX, queries.shape[1])
        hbm = pl.BlockSpec(memory_space=pltpu.HBM)
        out = pl.pallas_call(
            functools.partial(kernel, frames),
            out_shape=pltpu.VMEM(grid, jnp.bfloat16),
            in_specs=[hbm] * 5,
            out_specs=pl.BlockSpec(memory_space=pltpu.VMEM),
            scratch_shapes=[
                pltpu.VMEM((LOCAL,) + block, jnp.bfloat16),
                pltpu.VMEM((2, 3, LOCAL) + block, jnp.bfloat16),
                pltpu.VMEM(block, jnp.bfloat16),
                pltpu.VMEM((LOCAL,) + block, jnp.bfloat16),
                pltpu.SMEM((3, head_reach.shape[0]), jnp.int32),
                pltpu.SMEM((1, frames), jnp.int32),
                pltpu.SemaphoreType.DMA((3,)),
                pltpu.SemaphoreType.DMA((3, LOCAL)),
                pltpu.SemaphoreType.DMA((2, 2, LOCAL)),
                pltpu.SemaphoreType.DMA((2, 2, LOCAL)),
                pltpu.SemaphoreType.DMA,
                pltpu.SemaphoreType.DMA,
                pltpu.SemaphoreType.DMA((2,)),
                pltpu.SemaphoreType.REGULAR,
            ],
            compiler_params=pltpu.CompilerParams(
                collective_id=0, has_side_effects=True, vmem_limit_bytes=VMEM
            ),
        )(
            head_reach.T,
            frame_valid.reshape(1, frames),
            *(
                pltpu.with_memory_space_constraint(array.reshape(grid), pltpu.HBM)
                for array in (queries, keys, values)
            ),
        )
        return out.reshape(queries.shape)

    rows = P(("frame", "head"), None)
    return jax.shard_map(
        body, mesh=mesh, in_specs=(rows, rows, rows, P(), P()), out_specs=rows, check_vma=False
    )
```

```python
import functools
import math

import jax
import jax.numpy as jnp
from jax import lax
from jax.experimental import pallas as pl
from jax.experimental.pallas import tpu as pltpu
from jax.sharding import PartitionSpec as P

DH = 128
ROWS = 2
PAIRS = 5
PIX = 16
TW = 10
TILE = 8
LOCAL = 3
BLOCK = 8 * ROWS * PIX
VMEM = 62 * 2**20
MESH = pl.DeviceIdType.MESH
BIG = float(2**20)
SCALE = math.log2(math.e) / math.sqrt(DH)


def query_features(pair, reach_h, reach_w):
    shape = (BLOCK, DH)
    row = lax.broadcasted_iota(jnp.int32, shape, 0)
    col = lax.broadcasted_iota(jnp.int32, shape, 1)
    tile_y = row >> 7
    tile_x = 2 * pair + ((row & 15) >> 3)
    key_y = (col >= TW).astype(jnp.int32)
    key_x = col - TW * key_y
    size_y = jnp.minimum(2 * reach_h + 1, 2)
    size_x = jnp.minimum(2 * reach_w + 1, TW)
    low_y = jnp.clip(tile_y - reach_h, 0, 2 - size_y)
    low_x = jnp.clip(tile_x - reach_w, 0, TW - size_x)
    inside = (key_y >= low_y) & (key_y < low_y + size_y)
    inside = inside & (key_x >= low_x) & (key_x < low_x + size_x)
    return jnp.where(inside, jnp.float32(0.0), jnp.float32(-BIG))


def key_features(part, low, high):
    shape = (ROWS, PIX, DH)
    pix = lax.broadcasted_iota(jnp.int32, shape, 1)
    col = lax.broadcasted_iota(jnp.int32, shape, 2)
    tile = (part // 4) * TW + jnp.where(pix >= TILE, high, low)
    return jnp.where(col == tile, jnp.float32(1.0), jnp.float32(0.0)).astype(jnp.bfloat16)


def wait_bytes(ref, sem):
    pltpu.make_async_copy(ref, ref, sem).wait()


def kernel(
    frames, reach_hbm, valid_hbm, q_ref, k_ref, v_ref, out_ref,
    qbuf, kvbuf, kfeat, qfeat, upper, obuf, reach_ref, valid_ref,
    send_sem, in_sem, fwd_sem, halo_sem, out_send_sem, out_sem, small_sem, ready_sem,
):
    frame = lax.axis_index("frame")
    me = lax.axis_index("head")
    half = frames // 2

    def swap(index, at):
        return lax.rem(index + jnp.where(at >= half, 4, 0), 8)

    group = swap(me, frame)
    has_prev = frame > 0
    has_next = frame < frames - 1
    prev_id = {"frame": frame - 1, "head": swap(group, frame - 1)}
    next_id = {"frame": frame + 1, "head": swap(group, frame + 1)}

    def peer(step):
        part = lax.rem(me // 4 + step // 4, 2) * 4 + lax.rem(me + step, 4)
        return part

    barrier = pltpu.get_barrier_semaphore()
    for step in range(1, 8):
        pl.semaphore_signal(
            barrier, inc=1, device_id={"frame": frame, "head": peer(step)}, device_id_type=MESH
        )

    even = lax.rem(frame, 2) == 0
    odd = jnp.logical_not(even)

    def greet(sem, target):
        pl.semaphore_signal(sem, inc=1, device_id=target, device_id_type=MESH)

    @pl.when(has_prev)
    def _():
        greet(barrier, prev_id)

    @pl.when(even)
    def _():
        greet(barrier, next_id)

    pl.semaphore_wait(barrier, 8 + jnp.where(odd & has_next, 1, 0))

    @pl.when(odd & has_next)
    def _():
        greet(ready_sem, next_id)

    def cols(of_group, head):
        return pl.ds(pl.multiple_of((of_group * LOCAL + head) * DH, DH), DH)

    order = (5, 1, 4, 3, 6, 2, 7)

    def send(at, head):
        ref = (q_ref, k_ref, v_ref)[at]
        land = qbuf.at[head, me] if at == 0 else kvbuf.at[at - 1, 1, head, me]
        for step in order:
            target = peer(step)
            pltpu.make_async_remote_copy(
                src_ref=ref.at[:, :, :, cols(swap(target, frame), head)],
                dst_ref=land,
                send_sem=send_sem.at[at],
                recv_sem=in_sem.at[at, head],
                device_id={"frame": frame, "head": target},
                device_id_type=MESH,
            ).start()
        pltpu.make_async_copy(
            ref.at[:, :, :, cols(group, head)], land, in_sem.at[at, head]
        ).start()

    for at, head in ((1, 0), (2, 0), (0, 0), (1, 1), (2, 1), (1, 2), (2, 2), (0, 1), (0, 2)):
        send(at, head)

    reach_copy = pltpu.make_async_copy(reach_hbm, reach_ref, small_sem.at[0])
    valid_copy = pltpu.make_async_copy(valid_hbm, valid_ref, small_sem.at[1])
    reach_copy.start()
    valid_copy.start()

    for part in range(8):
        for pair in range(PAIRS):
            kfeat[part, :, pair] = key_features(part, 2 * pair, 2 * pair + 1)
        for pair in range(1, PAIRS - 1):
            kfeat[part, :, PAIRS - 1 + pair] = key_features(part, 2 * pair + 2, 2 * pair - 1)
    pix = lax.broadcasted_iota(jnp.int32, (PIX, DH), 0)
    upper[...] = jnp.where(pix >= TILE, jnp.float32(1.0), jnp.float32(0.0)).astype(jnp.bfloat16)

    @pl.when(jnp.logical_not(has_prev))
    def _():
        kvbuf[:, 0] = jnp.zeros(kvbuf.shape[:1] + kvbuf.shape[2:], jnp.bfloat16)

    @pl.when(jnp.logical_not(has_next))
    def _():
        kvbuf[:, 2] = jnp.zeros(kvbuf.shape[:1] + kvbuf.shape[2:], jnp.bfloat16)

    def forward(head, kv, way):
        return pltpu.make_async_remote_copy(
            src_ref=kvbuf.at[kv, 1, head],
            dst_ref=kvbuf.at[kv, 2 - 2 * way, head],
            send_sem=fwd_sem.at[kv, way, head],
            recv_sem=halo_sem.at[kv, way, head],
            device_id=(prev_id, next_id)[way],
            device_id_type=MESH,
        )

    def pass_on(head):
        for kv in range(2):
            wait_bytes(kvbuf.at[kv, 1, head], in_sem.at[kv + 1, head])

            @pl.when(has_prev)
            def _():
                forward(head, kv, 0).start()

            @pl.when(has_next)
            def _():
                forward(head, kv, 1).start()

    reach_copy.wait()
    valid_copy.wait()
    live_own = valid_ref[0, frame]
    live_prev = jnp.where(has_prev, valid_ref[0, jnp.maximum(frame - 1, 0)], 0)
    live_next = jnp.where(has_next, valid_ref[0, jnp.minimum(frame + 1, frames - 1)], 0)

    def mask_rows(head, carry):
        row = group * LOCAL + head
        near = reach_ref[0, row] >= 1
        allowed = ((live_prev > 0) & near, live_own > 0, (live_next > 0) & near)
        for pair in range(PAIRS):
            base = query_features(pair, reach_ref[1, row], reach_ref[2, row])
            for slot in range(3):
                level = jnp.where(allowed[slot], jnp.float32(0.0), jnp.float32(-BIG))
                qfeat[head, pair, slot] = jnp.minimum(base, level).astype(jnp.bfloat16)
        return carry

    lax.fori_loop(0, LOCAL, mask_rows, 0)

    def around(take, pair):
        if pair in (0, PAIRS - 1):
            both = (take(pair), take(abs(pair - 1)))
        else:
            is_upper = (upper[...] > 0)[None, None]
            both = (take(pair), jnp.where(is_upper, take(pair - 1), take(pair + 1)))
        return jnp.concatenate([block.reshape(BLOCK, DH) for block in both], axis=0)

    def score(head, pair):
        query = qbuf[head, :, :, pair].reshape(BLOCK, DH)
        second = abs(pair - 1) if pair in (0, PAIRS - 1) else PAIRS - 1 + pair
        tiles = jnp.concatenate(
            [kfeat[:, :, at].reshape(BLOCK, DH) for at in (pair, second)], axis=0
        )
        scores = []
        for slot in range(3):
            keys = around(lambda at: kvbuf[0, slot, head, :, :, at], pair)
            scores.append(
                lax.dot_general(
                    jnp.concatenate([query, qfeat[head, pair, slot]], axis=1),
                    jnp.concatenate([keys, tiles], axis=1),
                    (((1,), (1,)), ((), ())),
                    preferred_element_type=jnp.float32,
                )
            )
        return scores

    def mix(head, pair, scores):
        top = jnp.max(functools.reduce(jnp.maximum, scores), axis=1, keepdims=True)
        ones = jnp.ones((2 * BLOCK, DH), jnp.bfloat16)
        mixed = None
        for slot in range(3):
            weights = jnp.exp2((scores[slot] - top) * SCALE).astype(jnp.bfloat16)
            values = around(lambda at: kvbuf[1, slot, head, :, :, at], pair)
            term = jnp.dot(
                weights,
                jnp.concatenate([values, ones], axis=1),
                preferred_element_type=jnp.float32,
            )
            mixed = term if mixed is None else mixed + term
        result = mixed[:, :DH] / mixed[:, DH:]
        result = jnp.where(live_own > 0, result, jnp.float32(0.0)).astype(jnp.bfloat16)
        obuf[head, :, :, pair] = result.reshape(8, ROWS, PIX, DH)

    def send_out(head, first, last):
        landing = out_ref.at[:, first:last, :, cols(group, head)]
        for step in order:
            target = peer(step)
            pltpu.make_async_remote_copy(
                src_ref=obuf.at[head, target, :, first:last],
                dst_ref=landing,
                send_sem=out_send_sem,
                recv_sem=out_sem,
                device_id={"frame": frame, "head": target},
                device_id_type=MESH,
            ).start()
        pltpu.make_async_copy(obuf.at[head, me, :, first:last], landing, out_sem).start()

    @pl.when(even & has_prev)
    def _():
        pl.semaphore_wait(ready_sem, 1)

    pass_on(0)

    def per_head(head, carry):
        @pl.when(head < LOCAL - 1)
        def _():
            pass_on(head + 1)

        wait_bytes(qbuf.at[head], in_sem.at[0, head])
        for kv in range(2):

            @pl.when(has_next)
            def _():
                forward(head, kv, 0).wait_recv()

            @pl.when(has_prev)
            def _():
                forward(head, kv, 1).wait_recv()

        scores = score(head, 0)
        for pair in range(PAIRS):
            following = score(head, pair + 1) if pair + 1 < PAIRS else None
            mix(head, pair, scores)
            scores = following
            if pair in (2, PAIRS - 1):
                send_out(head, 0 if pair == 2 else 3, pair + 1)
        return carry

    lax.fori_loop(0, LOCAL, per_head, 0)

    for at in range(3):
        wait_bytes(qbuf.at[:, 0:7], send_sem.at[at])
    for head in range(LOCAL):
        for kv in range(2):

            @pl.when(has_prev)
            def _():
                forward(head, kv, 0).wait_send()

            @pl.when(has_next)
            def _():
                forward(head, kv, 1).wait_send()

    wait_bytes(obuf.at[:, 0:7], out_send_sem)
    wait_bytes(obuf, out_sem)


def solution(mesh):
    frames = mesh.shape["frame"]
    block = (8, ROWS, PAIRS, PIX, DH)

    def body(queries, keys, values, head_reach, frame_valid):
        grid = (ROWS, PAIRS, PIX, queries.shape[1])
        hbm = pl.BlockSpec(memory_space=pltpu.HBM)
        out = pl.pallas_call(
            functools.partial(kernel, frames),
            out_shape=pltpu.VMEM(grid, jnp.bfloat16),
            in_specs=[hbm] * 5,
            out_specs=pl.BlockSpec(memory_space=pltpu.VMEM),
            scratch_shapes=[
                pltpu.VMEM((LOCAL,) + block, jnp.bfloat16),
                pltpu.VMEM((2, 3, LOCAL) + block, jnp.bfloat16),
                pltpu.VMEM((8, ROWS, 2 * PAIRS - 2, PIX, DH), jnp.bfloat16),
                pltpu.VMEM((LOCAL, PAIRS, 3, BLOCK, DH), jnp.bfloat16),
                pltpu.VMEM((PIX, DH), jnp.bfloat16),
                pltpu.VMEM((LOCAL,) + block, jnp.bfloat16),
                pltpu.SMEM((3, head_reach.shape[0]), jnp.int32),
                pltpu.SMEM((1, frames), jnp.int32),
                pltpu.SemaphoreType.DMA((3,)),
                pltpu.SemaphoreType.DMA((3, LOCAL)),
                pltpu.SemaphoreType.DMA((2, 2, LOCAL)),
                pltpu.SemaphoreType.DMA((2, 2, LOCAL)),
                pltpu.SemaphoreType.DMA,
                pltpu.SemaphoreType.DMA,
                pltpu.SemaphoreType.DMA((2,)),
                pltpu.SemaphoreType.REGULAR,
            ],
            compiler_params=pltpu.CompilerParams(
                collective_id=0, has_side_effects=True, vmem_limit_bytes=VMEM
            ),
        )(
            head_reach.T,
            frame_valid.reshape(1, frames),
            *(
                pltpu.with_memory_space_constraint(array.reshape(grid), pltpu.HBM)
                for array in (queries, keys, values)
            ),
        )
        return out.reshape(queries.shape)

    rows = P(("frame", "head"), None)
    return jax.shard_map(
        body, mesh=mesh, in_specs=(rows, rows, rows, P(), P()), out_specs=rows, check_vma=False
    )
```

```python
import functools
import math

import jax
import jax.numpy as jnp
from jax import lax
from jax.experimental import pallas as pl
from jax.experimental.pallas import tpu as pltpu
from jax.sharding import PartitionSpec as P

DH = 128
ROWS = 2
PAIRS = 5
PIX = 16
TW = 10
TILE = 8
LOCAL = 3
BLOCK = 8 * ROWS * PIX
VMEM = 62 * 2**20
MESH = pl.DeviceIdType.MESH
BIG = float(2**20)
SCALE = math.log2(math.e) / math.sqrt(DH)


def query_features(pair, reach_h, reach_w):
    shape = (BLOCK, DH)
    row = lax.broadcasted_iota(jnp.int32, shape, 0)
    col = lax.broadcasted_iota(jnp.int32, shape, 1)
    tile_y = row >> 7
    tile_x = 2 * pair + ((row & 15) >> 3)
    key_y = (col >= TW).astype(jnp.int32)
    key_x = col - TW * key_y
    size_y = jnp.minimum(2 * reach_h + 1, 2)
    size_x = jnp.minimum(2 * reach_w + 1, TW)
    low_y = jnp.clip(tile_y - reach_h, 0, 2 - size_y)
    low_x = jnp.clip(tile_x - reach_w, 0, TW - size_x)
    inside = (key_y >= low_y) & (key_y < low_y + size_y)
    inside = inside & (key_x >= low_x) & (key_x < low_x + size_x)
    return jnp.where(inside, jnp.float32(0.0), jnp.float32(-BIG))


def key_features(part, low, high):
    shape = (ROWS, PIX, DH)
    pix = lax.broadcasted_iota(jnp.int32, shape, 1)
    col = lax.broadcasted_iota(jnp.int32, shape, 2)
    tile = (part // 4) * TW + jnp.where(pix >= TILE, high, low)
    return jnp.where(col == tile, jnp.float32(1.0), jnp.float32(0.0)).astype(jnp.bfloat16)


def wait_bytes(ref, sem):
    pltpu.make_async_copy(ref, ref, sem).wait()


def kernel(
    frames, reach_hbm, valid_hbm, q_ref, k_ref, v_ref, out_ref,
    qbuf, kvbuf, kfeat, qfeat, upper, obuf, reach_ref, valid_ref,
    send_sem, in_sem, fwd_sem, halo_sem, out_send_sem, out_sem, small_sem, ready_sem,
):
    frame = lax.axis_index("frame")
    me = lax.axis_index("head")
    half = frames // 2

    def swap(index, at):
        return lax.rem(index + jnp.where(at >= half, 4, 0), 8)

    group = swap(me, frame)
    has_prev = frame > 0
    has_next = frame < frames - 1
    prev_id = {"frame": frame - 1, "head": swap(group, frame - 1)}
    next_id = {"frame": frame + 1, "head": swap(group, frame + 1)}

    mirror = 1 - 2 * lax.rem(frame, 2)

    def peer(step):
        across = lax.rem(me // 4 + step // 4, 2) * 4
        return across + lax.rem(me + 4 + mirror * (step % 4), 4)

    barrier = pltpu.get_barrier_semaphore()
    for step in range(1, 8):
        pl.semaphore_signal(
            barrier, inc=1, device_id={"frame": frame, "head": peer(step)}, device_id_type=MESH
        )

    even = lax.rem(frame, 2) == 0
    odd = jnp.logical_not(even)

    def greet(sem, target):
        pl.semaphore_signal(sem, inc=1, device_id=target, device_id_type=MESH)

    @pl.when(has_prev)
    def _():
        greet(barrier, prev_id)

    @pl.when(even)
    def _():
        greet(barrier, next_id)

    pl.semaphore_wait(barrier, 8 + jnp.where(odd & has_next, 1, 0))

    @pl.when(odd & has_next)
    def _():
        greet(ready_sem, next_id)

    def cols(of_group, head):
        return pl.ds(pl.multiple_of((of_group * LOCAL + head) * DH, DH), DH)

    order = (5, 3, 4, 2, 7, 1, 6)

    def send(at, head):
        ref = (q_ref, k_ref, v_ref)[at]
        land = qbuf.at[head, me] if at == 0 else kvbuf.at[at - 1, 1, head, me]
        for step in order:
            target = peer(step)
            pltpu.make_async_remote_copy(
                src_ref=ref.at[:, :, :, cols(swap(target, frame), head)],
                dst_ref=land,
                send_sem=send_sem.at[at],
                recv_sem=in_sem.at[at, head],
                device_id={"frame": frame, "head": target},
                device_id_type=MESH,
            ).start()
        pltpu.make_async_copy(
            ref.at[:, :, :, cols(group, head)], land, in_sem.at[at, head]
        ).start()

    for at, head in ((1, 0), (2, 0), (0, 0), (1, 1), (2, 1), (1, 2), (2, 2), (0, 1), (0, 2)):
        send(at, head)

    reach_copy = pltpu.make_async_copy(reach_hbm, reach_ref, small_sem.at[0])
    valid_copy = pltpu.make_async_copy(valid_hbm, valid_ref, small_sem.at[1])
    reach_copy.start()
    valid_copy.start()

    for part in range(8):
        for pair in range(PAIRS):
            kfeat[part, :, pair] = key_features(part, 2 * pair, 2 * pair + 1)
        for pair in range(1, PAIRS - 1):
            kfeat[part, :, PAIRS - 1 + pair] = key_features(part, 2 * pair + 2, 2 * pair - 1)
    pix = lax.broadcasted_iota(jnp.int32, (PIX, DH), 0)
    upper[...] = jnp.where(pix >= TILE, jnp.float32(1.0), jnp.float32(0.0)).astype(jnp.bfloat16)

    @pl.when(jnp.logical_not(has_prev))
    def _():
        kvbuf[:, 0] = jnp.zeros(kvbuf.shape[:1] + kvbuf.shape[2:], jnp.bfloat16)

    @pl.when(jnp.logical_not(has_next))
    def _():
        kvbuf[:, 2] = jnp.zeros(kvbuf.shape[:1] + kvbuf.shape[2:], jnp.bfloat16)

    def forward(head, kv, way):
        return pltpu.make_async_remote_copy(
            src_ref=kvbuf.at[kv, 1, head],
            dst_ref=kvbuf.at[kv, 2 - 2 * way, head],
            send_sem=fwd_sem.at[kv, way, head],
            recv_sem=halo_sem.at[kv, way, head],
            device_id=(prev_id, next_id)[way],
            device_id_type=MESH,
        )

    def pass_on(head):
        for kv in range(2):
            wait_bytes(kvbuf.at[kv, 1, head], in_sem.at[kv + 1, head])

            @pl.when(has_prev)
            def _():
                forward(head, kv, 0).start()

            @pl.when(has_next)
            def _():
                forward(head, kv, 1).start()

    reach_copy.wait()
    valid_copy.wait()
    live_own = valid_ref[0, frame]
    live_prev = jnp.where(has_prev, valid_ref[0, jnp.maximum(frame - 1, 0)], 0)
    live_next = jnp.where(has_next, valid_ref[0, jnp.minimum(frame + 1, frames - 1)], 0)

    def mask_rows(head, carry):
        row = group * LOCAL + head
        near = reach_ref[0, row] >= 1
        allowed = ((live_prev > 0) & near, live_own > 0, (live_next > 0) & near)
        for pair in range(PAIRS):
            base = query_features(pair, reach_ref[1, row], reach_ref[2, row])
            for slot in range(3):
                level = jnp.where(allowed[slot], jnp.float32(0.0), jnp.float32(-BIG))
                qfeat[head, pair, slot] = jnp.minimum(base, level).astype(jnp.bfloat16)
        return carry

    lax.fori_loop(0, LOCAL, mask_rows, 0)

    def around(take, pair):
        if pair in (0, PAIRS - 1):
            both = (take(pair), take(abs(pair - 1)))
        else:
            is_upper = (upper[...] > 0)[None, None]
            both = (take(pair), jnp.where(is_upper, take(pair - 1), take(pair + 1)))
        return jnp.concatenate([block.reshape(BLOCK, DH) for block in both], axis=0)

    def score(head, pair):
        query = qbuf[head, :, :, pair].reshape(BLOCK, DH)
        second = abs(pair - 1) if pair in (0, PAIRS - 1) else PAIRS - 1 + pair
        tiles = jnp.concatenate(
            [kfeat[:, :, at].reshape(BLOCK, DH) for at in (pair, second)], axis=0
        )
        scores = []
        for slot in range(3):
            keys = around(lambda at: kvbuf[0, slot, head, :, :, at], pair)
            scores.append(
                lax.dot_general(
                    jnp.concatenate([query, qfeat[head, pair, slot]], axis=1),
                    jnp.concatenate([keys, tiles], axis=1),
                    (((1,), (1,)), ((), ())),
                    preferred_element_type=jnp.float32,
                )
            )
        return scores

    def mix(head, pair, scores):
        top = jnp.max(functools.reduce(jnp.maximum, scores), axis=1, keepdims=True)
        ones = jnp.ones((2 * BLOCK, DH), jnp.bfloat16)
        mixed = None
        for slot in range(3):
            weights = jnp.exp2((scores[slot] - top) * SCALE).astype(jnp.bfloat16)
            values = around(lambda at: kvbuf[1, slot, head, :, :, at], pair)
            term = jnp.dot(
                weights,
                jnp.concatenate([values, ones], axis=1),
                preferred_element_type=jnp.float32,
            )
            mixed = term if mixed is None else mixed + term
        result = mixed[:, :DH] / mixed[:, DH:]
        result = jnp.where(live_own > 0, result, jnp.float32(0.0)).astype(jnp.bfloat16)
        obuf[head, :, :, pair] = result.reshape(8, ROWS, PIX, DH)

    def send_out(head, first, last):
        landing = out_ref.at[:, first:last, :, cols(group, head)]
        for step in order:
            target = peer(step)
            pltpu.make_async_remote_copy(
                src_ref=obuf.at[head, target, :, first:last],
                dst_ref=landing,
                send_sem=out_send_sem,
                recv_sem=out_sem,
                device_id={"frame": frame, "head": target},
                device_id_type=MESH,
            ).start()
        pltpu.make_async_copy(obuf.at[head, me, :, first:last], landing, out_sem).start()

    @pl.when(even & has_prev)
    def _():
        pl.semaphore_wait(ready_sem, 1)

    pass_on(0)

    def per_head(head, carry):
        @pl.when(head < LOCAL - 1)
        def _():
            pass_on(head + 1)

        wait_bytes(qbuf.at[head], in_sem.at[0, head])
        for kv in range(2):

            @pl.when(has_next)
            def _():
                forward(head, kv, 0).wait_recv()

            @pl.when(has_prev)
            def _():
                forward(head, kv, 1).wait_recv()

        scores = score(head, 0)
        for pair in range(PAIRS):
            following = score(head, pair + 1) if pair + 1 < PAIRS else None
            mix(head, pair, scores)
            scores = following
            if pair in (1, 3, PAIRS - 1):
                send_out(head, pair // 2 * 2, pair + 1)
        return carry

    lax.fori_loop(0, LOCAL, per_head, 0)

    for at in range(3):
        wait_bytes(qbuf.at[:, 0:7], send_sem.at[at])
    for head in range(LOCAL):
        for kv in range(2):

            @pl.when(has_prev)
            def _():
                forward(head, kv, 0).wait_send()

            @pl.when(has_next)
            def _():
                forward(head, kv, 1).wait_send()

    wait_bytes(obuf.at[:, 0:7], out_send_sem)
    wait_bytes(obuf, out_sem)


def solution(mesh):
    frames = mesh.shape["frame"]
    block = (8, ROWS, PAIRS, PIX, DH)

    def body(queries, keys, values, head_reach, frame_valid):
        grid = (ROWS, PAIRS, PIX, queries.shape[1])
        hbm = pl.BlockSpec(memory_space=pltpu.HBM)
        out = pl.pallas_call(
            functools.partial(kernel, frames),
            out_shape=pltpu.VMEM(grid, jnp.bfloat16),
            in_specs=[hbm] * 5,
            out_specs=pl.BlockSpec(memory_space=pltpu.VMEM),
            scratch_shapes=[
                pltpu.VMEM((LOCAL,) + block, jnp.bfloat16),
                pltpu.VMEM((2, 3, LOCAL) + block, jnp.bfloat16),
                pltpu.VMEM((8, ROWS, 2 * PAIRS - 2, PIX, DH), jnp.bfloat16),
                pltpu.VMEM((LOCAL, PAIRS, 3, BLOCK, DH), jnp.bfloat16),
                pltpu.VMEM((PIX, DH), jnp.bfloat16),
                pltpu.VMEM((LOCAL,) + block, jnp.bfloat16),
                pltpu.SMEM((3, head_reach.shape[0]), jnp.int32),
                pltpu.SMEM((1, frames), jnp.int32),
                pltpu.SemaphoreType.DMA((3,)),
                pltpu.SemaphoreType.DMA((3, LOCAL)),
                pltpu.SemaphoreType.DMA((2, 2, LOCAL)),
                pltpu.SemaphoreType.DMA((2, 2, LOCAL)),
                pltpu.SemaphoreType.DMA,
                pltpu.SemaphoreType.DMA,
                pltpu.SemaphoreType.DMA((2,)),
                pltpu.SemaphoreType.REGULAR,
            ],
            compiler_params=pltpu.CompilerParams(
                collective_id=0, has_side_effects=True, vmem_limit_bytes=VMEM
            ),
        )(
            head_reach.T,
            frame_valid.reshape(1, frames),
            *(
                pltpu.with_memory_space_constraint(array.reshape(grid), pltpu.HBM)
                for array in (queries, keys, values)
            ),
        )
        return out.reshape(queries.shape)

    rows = P(("frame", "head"), None)
    return jax.shard_map(
        body, mesh=mesh, in_specs=(rows, rows, rows, P(), P()), out_specs=rows, check_vma=False
    )
```

```python
import functools
import math

import jax
import jax.numpy as jnp
from jax import lax
from jax.experimental import pallas as pl
from jax.experimental.pallas import tpu as pltpu
from jax.sharding import PartitionSpec as P

DH = 128
ROWS = 2
PAIRS = 5
PIX = 16
TW = 10
TILE = 8
LOCAL = 3
BLOCK = 8 * ROWS * PIX
VMEM = 62 * 2**20
MESH = pl.DeviceIdType.MESH
BIG = float(2**20)
SCALE = math.log2(math.e) / math.sqrt(DH)


def query_features(pair, reach_h, reach_w):
    shape = (BLOCK, DH)
    row = lax.broadcasted_iota(jnp.int32, shape, 0)
    col = lax.broadcasted_iota(jnp.int32, shape, 1)
    tile_y = row >> 7
    tile_x = 2 * pair + ((row & 15) >> 3)
    key_y = (col >= TW).astype(jnp.int32)
    key_x = col - TW * key_y
    size_y = jnp.minimum(2 * reach_h + 1, 2)
    size_x = jnp.minimum(2 * reach_w + 1, TW)
    low_y = jnp.clip(tile_y - reach_h, 0, 2 - size_y)
    low_x = jnp.clip(tile_x - reach_w, 0, TW - size_x)
    inside = (key_y >= low_y) & (key_y < low_y + size_y)
    inside = inside & (key_x >= low_x) & (key_x < low_x + size_x)
    return jnp.where(inside, jnp.float32(0.0), jnp.float32(-BIG))


def key_features(part, low, high):
    shape = (ROWS, PIX, DH)
    pix = lax.broadcasted_iota(jnp.int32, shape, 1)
    col = lax.broadcasted_iota(jnp.int32, shape, 2)
    tile = (part // 4) * TW + jnp.where(pix >= TILE, high, low)
    return jnp.where(col == tile, jnp.float32(1.0), jnp.float32(0.0)).astype(jnp.bfloat16)


def wait_bytes(ref, sem):
    pltpu.make_async_copy(ref, ref, sem).wait()


def kernel(
    frames, reach_hbm, valid_hbm, q_ref, k_ref, v_ref, out_ref,
    qbuf, kvbuf, kfeat, qfeat, upper, obuf, reach_ref, valid_ref,
    send_sem, in_sem, fwd_sem, halo_sem, out_send_sem, out_sem, small_sem, ready_sem,
):
    frame = lax.axis_index("frame")
    me = lax.axis_index("head")
    half = frames // 2

    def swap(index, at):
        return lax.rem(index + jnp.where(at >= half, 4, 0), 8)

    group = swap(me, frame)
    has_prev = frame > 0
    has_next = frame < frames - 1
    prev_id = {"frame": frame - 1, "head": swap(group, frame - 1)}
    next_id = {"frame": frame + 1, "head": swap(group, frame + 1)}

    def peer(step):
        part = lax.rem(me // 4 + step // 4, 2) * 4 + lax.rem(me + step, 4)
        return part

    barrier = pltpu.get_barrier_semaphore()
    for step in range(1, 8):
        pl.semaphore_signal(
            barrier, inc=1, device_id={"frame": frame, "head": peer(step)}, device_id_type=MESH
        )

    even = lax.rem(frame, 2) == 0
    odd = jnp.logical_not(even)
    below_turn = odd & (frame == half - 1)
    above_turn = even & (frame == half)
    odd_to_next = odd & has_next & jnp.logical_not(below_turn)
    even_to_prev = even & has_prev & jnp.logical_not(above_turn)

    def greet(sem, target):
        pl.semaphore_signal(sem, inc=1, device_id=target, device_id_type=MESH)

    def greet_or_answer(sem, to_mate, to_z, to_turn, mate, at_z, at_turn):
        @pl.when(to_mate)
        def _():
            greet(sem, mate)

        @pl.when(to_z)
        def _():
            greet(sem, at_z)

        @pl.when(to_turn)
        def _():
            greet(sem, at_turn)

    def count(*conditions):
        return sum(jnp.where(condition, 1, 0) for condition in conditions)

    greet_or_answer(barrier, odd, odd_to_next, above_turn, prev_id, next_id, prev_id)
    pl.semaphore_wait(barrier, 7 + count(even, even_to_prev, below_turn))
    greet_or_answer(ready_sem, even, even_to_prev, below_turn, next_id, prev_id, next_id)

    def cols(of_group, head):
        return pl.ds(pl.multiple_of((of_group * LOCAL + head) * DH, DH), DH)

    order = (5, 1, 4, 3, 6, 2, 7)

    def send(at, head):
        ref = (q_ref, k_ref, v_ref)[at]
        land = qbuf.at[head, me] if at == 0 else kvbuf.at[at - 1, 1, head, me]
        for step in order:
            target = peer(step)
            pltpu.make_async_remote_copy(
                src_ref=ref.at[:, :, :, cols(swap(target, frame), head)],
                dst_ref=land,
                send_sem=send_sem.at[at],
                recv_sem=in_sem.at[at, head],
                device_id={"frame": frame, "head": target},
                device_id_type=MESH,
            ).start()
        pltpu.make_async_copy(
            ref.at[:, :, :, cols(group, head)], land, in_sem.at[at, head]
        ).start()

    for at, head in ((1, 0), (2, 0), (0, 0), (1, 1), (2, 1), (1, 2), (2, 2), (0, 1), (0, 2)):
        send(at, head)

    reach_copy = pltpu.make_async_copy(reach_hbm, reach_ref, small_sem.at[0])
    valid_copy = pltpu.make_async_copy(valid_hbm, valid_ref, small_sem.at[1])
    reach_copy.start()
    valid_copy.start()

    for part in range(8):
        for pair in range(PAIRS):
            kfeat[part, :, pair] = key_features(part, 2 * pair, 2 * pair + 1)
        for pair in range(1, PAIRS - 1):
            kfeat[part, :, PAIRS - 1 + pair] = key_features(part, 2 * pair + 2, 2 * pair - 1)
    pix = lax.broadcasted_iota(jnp.int32, (PIX, DH), 0)
    upper[...] = jnp.where(pix >= TILE, jnp.float32(1.0), jnp.float32(0.0)).astype(jnp.bfloat16)

    @pl.when(jnp.logical_not(has_prev))
    def _():
        kvbuf[:, 0] = jnp.zeros(kvbuf.shape[:1] + kvbuf.shape[2:], jnp.bfloat16)

    @pl.when(jnp.logical_not(has_next))
    def _():
        kvbuf[:, 2] = jnp.zeros(kvbuf.shape[:1] + kvbuf.shape[2:], jnp.bfloat16)

    def forward(head, kv, way):
        return pltpu.make_async_remote_copy(
            src_ref=kvbuf.at[kv, 1, head],
            dst_ref=kvbuf.at[kv, 2 - 2 * way, head],
            send_sem=fwd_sem.at[kv, way, head],
            recv_sem=halo_sem.at[kv, way, head],
            device_id=(prev_id, next_id)[way],
            device_id_type=MESH,
        )

    def pass_on(head):
        for kv in range(2):
            wait_bytes(kvbuf.at[kv, 1, head], in_sem.at[kv + 1, head])

            @pl.when(has_prev)
            def _():
                forward(head, kv, 0).start()

            @pl.when(has_next)
            def _():
                forward(head, kv, 1).start()

    reach_copy.wait()
    valid_copy.wait()
    live_own = valid_ref[0, frame]
    live_prev = jnp.where(has_prev, valid_ref[0, jnp.maximum(frame - 1, 0)], 0)
    live_next = jnp.where(has_next, valid_ref[0, jnp.minimum(frame + 1, frames - 1)], 0)

    def mask_rows(head, carry):
        row = group * LOCAL + head
        near = reach_ref[0, row] >= 1
        allowed = ((live_prev > 0) & near, live_own > 0, (live_next > 0) & near)
        for pair in range(PAIRS):
            base = query_features(pair, reach_ref[1, row], reach_ref[2, row])
            for slot in range(3):
                level = jnp.where(allowed[slot], jnp.float32(0.0), jnp.float32(-BIG))
                qfeat[head, pair, slot] = jnp.minimum(base, level).astype(jnp.bfloat16)
        return carry

    lax.fori_loop(0, LOCAL, mask_rows, 0)

    def around(take, pair):
        if pair in (0, PAIRS - 1):
            both = (take(pair), take(abs(pair - 1)))
        else:
            is_upper = (upper[...] > 0)[None, None]
            both = (take(pair), jnp.where(is_upper, take(pair - 1), take(pair + 1)))
        return jnp.concatenate([block.reshape(BLOCK, DH) for block in both], axis=0)

    def score(head, pair):
        query = qbuf[head, :, :, pair].reshape(BLOCK, DH)
        second = abs(pair - 1) if pair in (0, PAIRS - 1) else PAIRS - 1 + pair
        tiles = jnp.concatenate(
            [kfeat[:, :, at].reshape(BLOCK, DH) for at in (pair, second)], axis=0
        )
        scores = []
        for slot in range(3):
            keys = around(lambda at: kvbuf[0, slot, head, :, :, at], pair)
            scores.append(
                lax.dot_general(
                    jnp.concatenate([query, qfeat[head, pair, slot]], axis=1),
                    jnp.concatenate([keys, tiles], axis=1),
                    (((1,), (1,)), ((), ())),
                    preferred_element_type=jnp.float32,
                )
            )
        return scores

    def mix(head, pair, scores):
        top = jnp.max(functools.reduce(jnp.maximum, scores), axis=1, keepdims=True)
        ones = jnp.ones((2 * BLOCK, DH), jnp.bfloat16)
        mixed = None
        for slot in range(3):
            weights = jnp.exp2((scores[slot] - top) * SCALE).astype(jnp.bfloat16)
            values = around(lambda at: kvbuf[1, slot, head, :, :, at], pair)
            term = jnp.dot(
                weights,
                jnp.concatenate([values, ones], axis=1),
                preferred_element_type=jnp.float32,
            )
            mixed = term if mixed is None else mixed + term
        result = mixed[:, :DH] / mixed[:, DH:]
        result = jnp.where(live_own > 0, result, jnp.float32(0.0)).astype(jnp.bfloat16)
        obuf[head, :, :, pair] = result.reshape(8, ROWS, PIX, DH)

    def send_out(head, first, last):
        landing = out_ref.at[:, first:last, :, cols(group, head)]
        for step in order:
            target = peer(step)
            pltpu.make_async_remote_copy(
                src_ref=obuf.at[head, target, :, first:last],
                dst_ref=landing,
                send_sem=out_send_sem,
                recv_sem=out_sem,
                device_id={"frame": frame, "head": target},
                device_id_type=MESH,
            ).start()
        pltpu.make_async_copy(obuf.at[head, me, :, first:last], landing, out_sem).start()

    @pl.when(odd | above_turn)
    def _():
        pl.semaphore_wait(ready_sem, count(odd, odd_to_next, above_turn))

    pass_on(0)

    def per_head(head, carry):
        @pl.when(head < LOCAL - 1)
        def _():
            pass_on(head + 1)

        wait_bytes(qbuf.at[head], in_sem.at[0, head])
        for kv in range(2):

            @pl.when(has_next)
            def _():
                forward(head, kv, 0).wait_recv()

            @pl.when(has_prev)
            def _():
                forward(head, kv, 1).wait_recv()

        scores = score(head, 0)
        for pair in range(PAIRS):
            following = score(head, pair + 1) if pair + 1 < PAIRS else None
            mix(head, pair, scores)
            scores = following
            if pair in (2, PAIRS - 1):
                send_out(head, 0 if pair == 2 else 3, pair + 1)
        return carry

    lax.fori_loop(0, LOCAL, per_head, 0)

    for at in range(3):
        wait_bytes(qbuf.at[:, 0:7], send_sem.at[at])
    for head in range(LOCAL):
        for kv in range(2):

            @pl.when(has_prev)
            def _():
                forward(head, kv, 0).wait_send()

            @pl.when(has_next)
            def _():
                forward(head, kv, 1).wait_send()

    wait_bytes(obuf.at[:, 0:7], out_send_sem)
    wait_bytes(obuf, out_sem)


def solution(mesh):
    frames = mesh.shape["frame"]
    block = (8, ROWS, PAIRS, PIX, DH)

    def body(queries, keys, values, head_reach, frame_valid):
        grid = (ROWS, PAIRS, PIX, queries.shape[1])
        hbm = pl.BlockSpec(memory_space=pltpu.HBM)
        out = pl.pallas_call(
            functools.partial(kernel, frames),
            out_shape=pltpu.VMEM(grid, jnp.bfloat16),
            in_specs=[hbm] * 5,
            out_specs=pl.BlockSpec(memory_space=pltpu.VMEM),
            scratch_shapes=[
                pltpu.VMEM((LOCAL,) + block, jnp.bfloat16),
                pltpu.VMEM((2, 3, LOCAL) + block, jnp.bfloat16),
                pltpu.VMEM((8, ROWS, 2 * PAIRS - 2, PIX, DH), jnp.bfloat16),
                pltpu.VMEM((LOCAL, PAIRS, 3, BLOCK, DH), jnp.bfloat16),
                pltpu.VMEM((PIX, DH), jnp.bfloat16),
                pltpu.VMEM((LOCAL,) + block, jnp.bfloat16),
                pltpu.SMEM((3, head_reach.shape[0]), jnp.int32),
                pltpu.SMEM((1, frames), jnp.int32),
                pltpu.SemaphoreType.DMA((3,)),
                pltpu.SemaphoreType.DMA((3, LOCAL)),
                pltpu.SemaphoreType.DMA((2, 2, LOCAL)),
                pltpu.SemaphoreType.DMA((2, 2, LOCAL)),
                pltpu.SemaphoreType.DMA,
                pltpu.SemaphoreType.DMA,
                pltpu.SemaphoreType.DMA((2,)),
                pltpu.SemaphoreType.REGULAR,
            ],
            compiler_params=pltpu.CompilerParams(
                collective_id=0, has_side_effects=True, vmem_limit_bytes=VMEM
            ),
        )(
            head_reach.T,
            frame_valid.reshape(1, frames),
            *(
                pltpu.with_memory_space_constraint(array.reshape(grid), pltpu.HBM)
                for array in (queries, keys, values)
            ),
        )
        return out.reshape(queries.shape)

    rows = P(("frame", "head"), None)
    return jax.shard_map(
        body, mesh=mesh, in_specs=(rows, rows, rows, P(), P()), out_specs=rows, check_vma=False
    )
```

```python
import functools
import math

import jax
import jax.numpy as jnp
from jax import lax
from jax.experimental import pallas as pl
from jax.experimental.pallas import tpu as pltpu
from jax.sharding import PartitionSpec as P

DH = 128
ROWS = 2
PAIRS = 5
PIX = 16
TW = 10
TILE = 8
LOCAL = 3
BLOCK = 8 * ROWS * PIX
VMEM = 62 * 2**20
MESH = pl.DeviceIdType.MESH
BIG = float(2**20)
SCALE = math.log2(math.e) / math.sqrt(DH)


def query_features(pair, reach_h, reach_w):
    shape = (BLOCK, DH)
    row = lax.broadcasted_iota(jnp.int32, shape, 0)
    col = lax.broadcasted_iota(jnp.int32, shape, 1)
    tile_y = row >> 7
    tile_x = 2 * pair + ((row & 15) >> 3)
    key_y = (col >= TW).astype(jnp.int32)
    key_x = col - TW * key_y
    size_y = jnp.minimum(2 * reach_h + 1, 2)
    size_x = jnp.minimum(2 * reach_w + 1, TW)
    low_y = jnp.clip(tile_y - reach_h, 0, 2 - size_y)
    low_x = jnp.clip(tile_x - reach_w, 0, TW - size_x)
    inside = (key_y >= low_y) & (key_y < low_y + size_y)
    inside = inside & (key_x >= low_x) & (key_x < low_x + size_x)
    return jnp.where(inside, jnp.float32(0.0), jnp.float32(-BIG))


def key_features(part, low, high):
    shape = (ROWS, PIX, DH)
    pix = lax.broadcasted_iota(jnp.int32, shape, 1)
    col = lax.broadcasted_iota(jnp.int32, shape, 2)
    tile = (part // 4) * TW + jnp.where(pix >= TILE, high, low)
    return jnp.where(col == tile, jnp.float32(1.0), jnp.float32(0.0)).astype(jnp.bfloat16)


def wait_bytes(ref, sem):
    pltpu.make_async_copy(ref, ref, sem).wait()


def kernel(
    frames, reach_hbm, valid_hbm, q_ref, k_ref, v_ref, out_ref,
    qbuf, kvbuf, kfeat, qfeat, upper, obuf, reach_ref, valid_ref,
    send_sem, in_sem, fwd_sem, halo_sem, out_send_sem, out_sem, small_sem, ready_sem,
):
    frame = lax.axis_index("frame")
    me = lax.axis_index("head")
    half = frames // 2

    def swap(index, at):
        return lax.rem(index + jnp.where(at >= half, 4, 0), 8)

    group = swap(me, frame)
    has_prev = frame > 0
    has_next = frame < frames - 1
    prev_id = {"frame": frame - 1, "head": swap(group, frame - 1)}
    next_id = {"frame": frame + 1, "head": swap(group, frame + 1)}

    def peer(step):
        part = lax.rem(me // 4 + step // 4, 2) * 4 + lax.rem(me + step, 4)
        return part

    barrier = pltpu.get_barrier_semaphore()
    for step in range(1, 8):
        pl.semaphore_signal(
            barrier, inc=1, device_id={"frame": frame, "head": peer(step)}, device_id_type=MESH
        )

    even = lax.rem(frame, 2) == 0
    odd = jnp.logical_not(even)
    below_turn = odd & (frame == half - 1)
    above_turn = even & (frame == half)
    odd_to_next = odd & has_next & jnp.logical_not(below_turn)
    even_to_prev = even & has_prev & jnp.logical_not(above_turn)

    def greet(sem, target):
        pl.semaphore_signal(sem, inc=1, device_id=target, device_id_type=MESH)

    def greet_or_answer(sem, to_mate, to_z, to_turn, mate, at_z, at_turn):
        @pl.when(to_mate)
        def _():
            greet(sem, mate)

        @pl.when(to_z)
        def _():
            greet(sem, at_z)

        @pl.when(to_turn)
        def _():
            greet(sem, at_turn)

    def count(*conditions):
        return sum(jnp.where(condition, 1, 0) for condition in conditions)

    greet_or_answer(barrier, odd, odd_to_next, above_turn, prev_id, next_id, prev_id)
    pl.semaphore_wait(barrier, 7 + count(even, even_to_prev, below_turn))
    greet_or_answer(ready_sem, even, even_to_prev, below_turn, next_id, prev_id, next_id)

    def cols(of_group, head):
        return pl.ds(pl.multiple_of((of_group * LOCAL + head) * DH, DH), DH)

    order = (5, 1, 4, 3, 6, 2, 7)

    def send(at, head):
        ref = (q_ref, k_ref, v_ref)[at]
        land = qbuf.at[head, me] if at == 0 else kvbuf.at[at - 1, 1, head, me]
        for step in order:
            target = peer(step)
            pltpu.make_async_remote_copy(
                src_ref=ref.at[:, :, :, cols(swap(target, frame), head)],
                dst_ref=land,
                send_sem=send_sem.at[at],
                recv_sem=in_sem.at[at, head],
                device_id={"frame": frame, "head": target},
                device_id_type=MESH,
            ).start()
        pltpu.make_async_copy(
            ref.at[:, :, :, cols(group, head)], land, in_sem.at[at, head]
        ).start()

    for at, head in ((1, 0), (2, 0), (0, 0), (1, 1), (2, 1), (1, 2), (2, 2), (0, 1), (0, 2)):
        send(at, head)

    reach_copy = pltpu.make_async_copy(reach_hbm, reach_ref, small_sem.at[0])
    valid_copy = pltpu.make_async_copy(valid_hbm, valid_ref, small_sem.at[1])
    reach_copy.start()
    valid_copy.start()

    for part in range(8):
        for pair in range(PAIRS):
            kfeat[part, :, pair] = key_features(part, 2 * pair, 2 * pair + 1)
        for pair in range(1, PAIRS - 1):
            kfeat[part, :, PAIRS - 1 + pair] = key_features(part, 2 * pair + 2, 2 * pair - 1)
    pix = lax.broadcasted_iota(jnp.int32, (PIX, DH), 0)
    upper[...] = jnp.where(pix >= TILE, jnp.float32(1.0), jnp.float32(0.0)).astype(jnp.bfloat16)

    @pl.when(jnp.logical_not(has_prev))
    def _():
        kvbuf[:, 0] = jnp.zeros(kvbuf.shape[:1] + kvbuf.shape[2:], jnp.bfloat16)

    @pl.when(jnp.logical_not(has_next))
    def _():
        kvbuf[:, 2] = jnp.zeros(kvbuf.shape[:1] + kvbuf.shape[2:], jnp.bfloat16)

    def forward(head, kv, way):
        return pltpu.make_async_remote_copy(
            src_ref=kvbuf.at[kv, 1, head],
            dst_ref=kvbuf.at[kv, 2 - 2 * way, head],
            send_sem=fwd_sem.at[kv, way, head],
            recv_sem=halo_sem.at[kv, way, head],
            device_id=(prev_id, next_id)[way],
            device_id_type=MESH,
        )

    def pass_on(head):
        for kv in range(2):
            wait_bytes(kvbuf.at[kv, 1, head], in_sem.at[kv + 1, head])

            @pl.when(even & has_prev)
            def _():
                forward(head, kv, 0).start()

            @pl.when(odd & has_next)
            def _():
                forward(head, kv, 1).start()

        for kv in range(2):

            @pl.when(even)
            def _():
                forward(head, kv, 1).start()

            @pl.when(odd)
            def _():
                forward(head, kv, 0).start()

    reach_copy.wait()
    valid_copy.wait()
    live_own = valid_ref[0, frame]
    live_prev = jnp.where(has_prev, valid_ref[0, jnp.maximum(frame - 1, 0)], 0)
    live_next = jnp.where(has_next, valid_ref[0, jnp.minimum(frame + 1, frames - 1)], 0)

    def mask_rows(head, carry):
        row = group * LOCAL + head
        near = reach_ref[0, row] >= 1
        allowed = ((live_prev > 0) & near, live_own > 0, (live_next > 0) & near)
        for pair in range(PAIRS):
            base = query_features(pair, reach_ref[1, row], reach_ref[2, row])
            for slot in range(3):
                level = jnp.where(allowed[slot], jnp.float32(0.0), jnp.float32(-BIG))
                qfeat[head, pair, slot] = jnp.minimum(base, level).astype(jnp.bfloat16)
        return carry

    lax.fori_loop(0, LOCAL, mask_rows, 0)

    def around(take, pair):
        if pair in (0, PAIRS - 1):
            both = (take(pair), take(abs(pair - 1)))
        else:
            is_upper = (upper[...] > 0)[None, None]
            both = (take(pair), jnp.where(is_upper, take(pair - 1), take(pair + 1)))
        return jnp.concatenate([block.reshape(BLOCK, DH) for block in both], axis=0)

    def score(head, pair):
        query = qbuf[head, :, :, pair].reshape(BLOCK, DH)
        second = abs(pair - 1) if pair in (0, PAIRS - 1) else PAIRS - 1 + pair
        tiles = jnp.concatenate(
            [kfeat[:, :, at].reshape(BLOCK, DH) for at in (pair, second)], axis=0
        )
        scores = []
        for slot in range(3):
            keys = around(lambda at: kvbuf[0, slot, head, :, :, at], pair)
            scores.append(
                lax.dot_general(
                    jnp.concatenate([query, qfeat[head, pair, slot]], axis=1),
                    jnp.concatenate([keys, tiles], axis=1),
                    (((1,), (1,)), ((), ())),
                    preferred_element_type=jnp.float32,
                )
            )
        return scores

    def mix(head, pair, scores):
        top = jnp.max(functools.reduce(jnp.maximum, scores), axis=1, keepdims=True)
        ones = jnp.ones((2 * BLOCK, DH), jnp.bfloat16)
        mixed = None
        for slot in range(3):
            weights = jnp.exp2((scores[slot] - top) * SCALE).astype(jnp.bfloat16)
            values = around(lambda at: kvbuf[1, slot, head, :, :, at], pair)
            term = jnp.dot(
                weights,
                jnp.concatenate([values, ones], axis=1),
                preferred_element_type=jnp.float32,
            )
            mixed = term if mixed is None else mixed + term
        result = mixed[:, :DH] / mixed[:, DH:]
        result = jnp.where(live_own > 0, result, jnp.float32(0.0)).astype(jnp.bfloat16)
        obuf[head, :, :, pair] = result.reshape(8, ROWS, PIX, DH)

    def send_out(head, first, last):
        landing = out_ref.at[:, first:last, :, cols(group, head)]
        for step in order:
            target = peer(step)
            pltpu.make_async_remote_copy(
                src_ref=obuf.at[head, target, :, first:last],
                dst_ref=landing,
                send_sem=out_send_sem,
                recv_sem=out_sem,
                device_id={"frame": frame, "head": target},
                device_id_type=MESH,
            ).start()
        pltpu.make_async_copy(obuf.at[head, me, :, first:last], landing, out_sem).start()

    @pl.when(odd | above_turn)
    def _():
        pl.semaphore_wait(ready_sem, count(odd, odd_to_next, above_turn))

    pass_on(0)

    def per_head(head, carry):
        @pl.when(head < LOCAL - 1)
        def _():
            pass_on(head + 1)

        wait_bytes(qbuf.at[head], in_sem.at[0, head])
        for kv in range(2):

            @pl.when(has_next)
            def _():
                forward(head, kv, 0).wait_recv()

            @pl.when(has_prev)
            def _():
                forward(head, kv, 1).wait_recv()

        scores = score(head, 0)
        for pair in range(PAIRS):
            following = score(head, pair + 1) if pair + 1 < PAIRS else None
            mix(head, pair, scores)
            scores = following
            if pair in (2, PAIRS - 1):
                send_out(head, 0 if pair == 2 else 3, pair + 1)
        return carry

    lax.fori_loop(0, LOCAL, per_head, 0)

    for at in range(3):
        wait_bytes(qbuf.at[:, 0:7], send_sem.at[at])
    for head in range(LOCAL):
        for kv in range(2):

            @pl.when(has_prev)
            def _():
                forward(head, kv, 0).wait_send()

            @pl.when(has_next)
            def _():
                forward(head, kv, 1).wait_send()

    wait_bytes(obuf.at[:, 0:7], out_send_sem)
    wait_bytes(obuf, out_sem)


def solution(mesh):
    frames = mesh.shape["frame"]
    block = (8, ROWS, PAIRS, PIX, DH)

    def body(queries, keys, values, head_reach, frame_valid):
        grid = (ROWS, PAIRS, PIX, queries.shape[1])
        hbm = pl.BlockSpec(memory_space=pltpu.HBM)
        out = pl.pallas_call(
            functools.partial(kernel, frames),
            out_shape=pltpu.VMEM(grid, jnp.bfloat16),
            in_specs=[hbm] * 5,
            out_specs=pl.BlockSpec(memory_space=pltpu.VMEM),
            scratch_shapes=[
                pltpu.VMEM((LOCAL,) + block, jnp.bfloat16),
                pltpu.VMEM((2, 3, LOCAL) + block, jnp.bfloat16),
                pltpu.VMEM((8, ROWS, 2 * PAIRS - 2, PIX, DH), jnp.bfloat16),
                pltpu.VMEM((LOCAL, PAIRS, 3, BLOCK, DH), jnp.bfloat16),
                pltpu.VMEM((PIX, DH), jnp.bfloat16),
                pltpu.VMEM((LOCAL,) + block, jnp.bfloat16),
                pltpu.SMEM((3, head_reach.shape[0]), jnp.int32),
                pltpu.SMEM((1, frames), jnp.int32),
                pltpu.SemaphoreType.DMA((3,)),
                pltpu.SemaphoreType.DMA((3, LOCAL)),
                pltpu.SemaphoreType.DMA((2, 2, LOCAL)),
                pltpu.SemaphoreType.DMA((2, 2, LOCAL)),
                pltpu.SemaphoreType.DMA,
                pltpu.SemaphoreType.DMA,
                pltpu.SemaphoreType.DMA((2,)),
                pltpu.SemaphoreType.REGULAR,
            ],
            compiler_params=pltpu.CompilerParams(
                collective_id=0, has_side_effects=True, vmem_limit_bytes=VMEM
            ),
        )(
            head_reach.T,
            frame_valid.reshape(1, frames),
            *(
                pltpu.with_memory_space_constraint(array.reshape(grid), pltpu.HBM)
                for array in (queries, keys, values)
            ),
        )
        return out.reshape(queries.shape)

    rows = P(("frame", "head"), None)
    return jax.shard_map(
        body, mesh=mesh, in_specs=(rows, rows, rows, P(), P()), out_specs=rows, check_vma=False
    )
```

```python
import functools
import math

import jax
import jax.numpy as jnp
from jax import lax
from jax.experimental import pallas as pl
from jax.experimental.pallas import tpu as pltpu
from jax.sharding import PartitionSpec as P

DH = 128
ROWS = 2
PAIRS = 5
PIX = 16
TW = 10
TILE = 8
LOCAL = 3
BLOCK = 8 * ROWS * PIX
VMEM = 62 * 2**20
MESH = pl.DeviceIdType.MESH
BIG = float(2**20)
SCALE = math.log2(math.e) / math.sqrt(DH)


def query_features(pair, reach_h, reach_w):
    shape = (BLOCK, DH)
    row = lax.broadcasted_iota(jnp.int32, shape, 0)
    col = lax.broadcasted_iota(jnp.int32, shape, 1)
    tile_y = row >> 7
    tile_x = 2 * pair + ((row & 15) >> 3)
    key_y = (col >= TW).astype(jnp.int32)
    key_x = col - TW * key_y
    size_y = jnp.minimum(2 * reach_h + 1, 2)
    size_x = jnp.minimum(2 * reach_w + 1, TW)
    low_y = jnp.clip(tile_y - reach_h, 0, 2 - size_y)
    low_x = jnp.clip(tile_x - reach_w, 0, TW - size_x)
    inside = (key_y >= low_y) & (key_y < low_y + size_y)
    inside = inside & (key_x >= low_x) & (key_x < low_x + size_x)
    return jnp.where(inside, jnp.float32(0.0), jnp.float32(-BIG))


def key_features(part, low, high):
    shape = (ROWS, PIX, DH)
    pix = lax.broadcasted_iota(jnp.int32, shape, 1)
    col = lax.broadcasted_iota(jnp.int32, shape, 2)
    tile = (part // 4) * TW + jnp.where(pix >= TILE, high, low)
    return jnp.where(col == tile, jnp.float32(1.0), jnp.float32(0.0)).astype(jnp.bfloat16)


def wait_bytes(ref, sem):
    pltpu.make_async_copy(ref, ref, sem).wait()


def kernel(
    frames, reach_hbm, valid_hbm, q_ref, k_ref, v_ref, out_ref,
    qbuf, kvbuf, kfeat, qfeat, upper, obuf, reach_ref, valid_ref,
    send_sem, in_sem, fwd_sem, halo_sem, out_send_sem, out_sem, small_sem, ready_sem,
):
    frame = lax.axis_index("frame")
    me = lax.axis_index("head")
    half = frames // 2

    def swap(index, at):
        return lax.rem(index + jnp.where(at >= half, 4, 0), 8)

    group = swap(me, frame)
    has_prev = frame > 0
    has_next = frame < frames - 1
    prev_id = {"frame": frame - 1, "head": swap(group, frame - 1)}
    next_id = {"frame": frame + 1, "head": swap(group, frame + 1)}

    def peer(step):
        part = lax.rem(me // 4 + step // 4, 2) * 4 + lax.rem(me + step, 4)
        return part

    barrier = pltpu.get_barrier_semaphore()
    for step in range(1, 8):
        pl.semaphore_signal(
            barrier, inc=1, device_id={"frame": frame, "head": peer(step)}, device_id_type=MESH
        )

    even = lax.rem(frame, 2) == 0
    odd = jnp.logical_not(even)
    below_turn = odd & (frame == half - 1)
    above_turn = even & (frame == half)
    odd_to_next = odd & has_next & jnp.logical_not(below_turn)
    even_to_prev = even & has_prev & jnp.logical_not(above_turn)

    def greet(sem, target):
        pl.semaphore_signal(sem, inc=1, device_id=target, device_id_type=MESH)

    def greet_or_answer(sem, to_mate, to_z, to_turn, mate, at_z, at_turn):
        @pl.when(to_mate)
        def _():
            greet(sem, mate)

        @pl.when(to_z)
        def _():
            greet(sem, at_z)

        @pl.when(to_turn)
        def _():
            greet(sem, at_turn)

    def count(*conditions):
        return sum(jnp.where(condition, 1, 0) for condition in conditions)

    greet_or_answer(barrier, odd, odd_to_next, above_turn, prev_id, next_id, prev_id)
    pl.semaphore_wait(barrier, 7 + count(even, even_to_prev, below_turn))
    greet_or_answer(ready_sem, even, even_to_prev, below_turn, next_id, prev_id, next_id)

    def cols(of_group, head):
        return pl.ds(pl.multiple_of((of_group * LOCAL + head) * DH, DH), DH)

    order = (5, 1, 4, 3, 6, 2, 7)

    def send(at, head):
        ref = (q_ref, k_ref, v_ref)[at]
        land = qbuf.at[head, me] if at == 0 else kvbuf.at[at - 1, 1, head, me]
        for step in order:
            target = peer(step)
            pltpu.make_async_remote_copy(
                src_ref=ref.at[:, :, :, cols(swap(target, frame), head)],
                dst_ref=land,
                send_sem=send_sem.at[at],
                recv_sem=in_sem.at[at, head],
                device_id={"frame": frame, "head": target},
                device_id_type=MESH,
            ).start()
        pltpu.make_async_copy(
            ref.at[:, :, :, cols(group, head)], land, in_sem.at[at, head]
        ).start()

    for at, head in ((1, 0), (2, 0), (0, 0), (1, 1), (2, 1), (1, 2), (2, 2), (0, 1), (0, 2)):
        send(at, head)

    reach_copy = pltpu.make_async_copy(reach_hbm, reach_ref, small_sem.at[0])
    valid_copy = pltpu.make_async_copy(valid_hbm, valid_ref, small_sem.at[1])
    reach_copy.start()
    valid_copy.start()

    for part in range(8):
        for pair in range(PAIRS):
            kfeat[part, :, pair] = key_features(part, 2 * pair, 2 * pair + 1)
        for pair in range(1, PAIRS - 1):
            kfeat[part, :, PAIRS - 1 + pair] = key_features(part, 2 * pair + 2, 2 * pair - 1)
    pix = lax.broadcasted_iota(jnp.int32, (PIX, DH), 0)
    upper[...] = jnp.where(pix >= TILE, jnp.float32(1.0), jnp.float32(0.0)).astype(jnp.bfloat16)

    @pl.when(jnp.logical_not(has_prev))
    def _():
        kvbuf[:, 0] = jnp.zeros(kvbuf.shape[:1] + kvbuf.shape[2:], jnp.bfloat16)

    @pl.when(jnp.logical_not(has_next))
    def _():
        kvbuf[:, 2] = jnp.zeros(kvbuf.shape[:1] + kvbuf.shape[2:], jnp.bfloat16)

    def forward(head, kv, way):
        return pltpu.make_async_remote_copy(
            src_ref=kvbuf.at[kv, 1, head],
            dst_ref=kvbuf.at[kv, 2 - 2 * way, head],
            send_sem=fwd_sem.at[kv, way, head],
            recv_sem=halo_sem.at[kv, way, head],
            device_id=(prev_id, next_id)[way],
            device_id_type=MESH,
        )

    def pass_on(head):
        for kv in range(2):
            wait_bytes(kvbuf.at[kv, 1, head], in_sem.at[kv + 1, head])

            @pl.when(even & has_prev)
            def _():
                forward(head, kv, 0).start()

            @pl.when(odd & has_next)
            def _():
                forward(head, kv, 1).start()

        for kv in range(2):

            @pl.when(even)
            def _():
                forward(head, kv, 1).start()

            @pl.when(odd)
            def _():
                forward(head, kv, 0).start()

    reach_copy.wait()
    valid_copy.wait()
    live_own = valid_ref[0, frame]
    live_prev = jnp.where(has_prev, valid_ref[0, jnp.maximum(frame - 1, 0)], 0)
    live_next = jnp.where(has_next, valid_ref[0, jnp.minimum(frame + 1, frames - 1)], 0)

    def mask_rows(head, carry):
        row = group * LOCAL + head
        near = reach_ref[0, row] >= 1
        allowed = ((live_prev > 0) & near, live_own > 0, (live_next > 0) & near)
        for pair in range(PAIRS):
            base = query_features(pair, reach_ref[1, row], reach_ref[2, row])
            for slot in range(3):
                level = jnp.where(allowed[slot], jnp.float32(0.0), jnp.float32(-BIG))
                qfeat[head, pair, slot] = jnp.minimum(base, level).astype(jnp.bfloat16)
        return carry

    lax.fori_loop(0, LOCAL, mask_rows, 0)

    def around(take, pair):
        if pair in (0, PAIRS - 1):
            both = (take(pair), take(abs(pair - 1)))
        else:
            is_upper = (upper[...] > 0)[None, None]
            both = (take(pair), jnp.where(is_upper, take(pair - 1), take(pair + 1)))
        return jnp.concatenate([block.reshape(BLOCK, DH) for block in both], axis=0)

    def score(head, pair):
        query = qbuf[head, :, :, pair].reshape(BLOCK, DH)
        second = abs(pair - 1) if pair in (0, PAIRS - 1) else PAIRS - 1 + pair
        tiles = jnp.concatenate(
            [kfeat[:, :, at].reshape(BLOCK, DH) for at in (pair, second)], axis=0
        )
        scores = []
        for slot in range(3):
            keys = around(lambda at: kvbuf[0, slot, head, :, :, at], pair)
            scores.append(
                lax.dot_general(
                    jnp.concatenate([query, qfeat[head, pair, slot]], axis=1),
                    jnp.concatenate([keys, tiles], axis=1),
                    (((1,), (1,)), ((), ())),
                    preferred_element_type=jnp.float32,
                )
            )
        return scores

    def mix(head, pair, scores):
        top = jnp.max(functools.reduce(jnp.maximum, scores), axis=1, keepdims=True)
        ones = jnp.ones((2 * BLOCK, DH), jnp.bfloat16)
        mixed = None
        for slot in range(3):
            weights = jnp.exp2((scores[slot] - top) * SCALE).astype(jnp.bfloat16)
            values = around(lambda at: kvbuf[1, slot, head, :, :, at], pair)
            term = jnp.dot(
                weights,
                jnp.concatenate([values, ones], axis=1),
                preferred_element_type=jnp.float32,
            )
            mixed = term if mixed is None else mixed + term
        result = mixed[:, :DH] / mixed[:, DH:]
        result = jnp.where(live_own > 0, result, jnp.float32(0.0)).astype(jnp.bfloat16)
        obuf[head, :, :, pair] = result.reshape(8, ROWS, PIX, DH)

    def send_out(head, first, last):
        landing = out_ref.at[:, first:last, :, cols(group, head)]
        for step in order:
            target = peer(step)
            pltpu.make_async_remote_copy(
                src_ref=obuf.at[head, target, :, first:last],
                dst_ref=landing,
                send_sem=out_send_sem,
                recv_sem=out_sem,
                device_id={"frame": frame, "head": target},
                device_id_type=MESH,
            ).start()
        pltpu.make_async_copy(obuf.at[head, me, :, first:last], landing, out_sem).start()

    @pl.when(odd | above_turn)
    def _():
        pl.semaphore_wait(ready_sem, count(odd, odd_to_next, above_turn))

    pass_on(0)

    def per_head(head, carry):
        @pl.when(head == 1)
        def _():
            pass_on(2)

        wait_bytes(qbuf.at[head], in_sem.at[0, head])
        for kv in range(2):

            @pl.when(has_next)
            def _():
                forward(head, kv, 0).wait_recv()

            @pl.when(has_prev)
            def _():
                forward(head, kv, 1).wait_recv()

        scores = score(head, 0)
        for pair in range(PAIRS):
            following = score(head, pair + 1) if pair + 1 < PAIRS else None
            mix(head, pair, scores)
            scores = following
            if pair == 1:

                @pl.when(head == 0)
                def _():
                    pass_on(1)

            if pair in (2, PAIRS - 1):
                send_out(head, 0 if pair == 2 else 3, pair + 1)
        return carry

    lax.fori_loop(0, LOCAL, per_head, 0)

    for at in range(3):
        wait_bytes(qbuf.at[:, 0:7], send_sem.at[at])
    for head in range(LOCAL):
        for kv in range(2):

            @pl.when(has_prev)
            def _():
                forward(head, kv, 0).wait_send()

            @pl.when(has_next)
            def _():
                forward(head, kv, 1).wait_send()

    wait_bytes(obuf.at[:, 0:7], out_send_sem)
    wait_bytes(obuf, out_sem)


def solution(mesh):
    frames = mesh.shape["frame"]
    block = (8, ROWS, PAIRS, PIX, DH)

    def body(queries, keys, values, head_reach, frame_valid):
        grid = (ROWS, PAIRS, PIX, queries.shape[1])
        hbm = pl.BlockSpec(memory_space=pltpu.HBM)
        out = pl.pallas_call(
            functools.partial(kernel, frames),
            out_shape=pltpu.VMEM(grid, jnp.bfloat16),
            in_specs=[hbm] * 5,
            out_specs=pl.BlockSpec(memory_space=pltpu.VMEM),
            scratch_shapes=[
                pltpu.VMEM((LOCAL,) + block, jnp.bfloat16),
                pltpu.VMEM((2, 3, LOCAL) + block, jnp.bfloat16),
                pltpu.VMEM((8, ROWS, 2 * PAIRS - 2, PIX, DH), jnp.bfloat16),
                pltpu.VMEM((LOCAL, PAIRS, 3, BLOCK, DH), jnp.bfloat16),
                pltpu.VMEM((PIX, DH), jnp.bfloat16),
                pltpu.VMEM((LOCAL,) + block, jnp.bfloat16),
                pltpu.SMEM((3, head_reach.shape[0]), jnp.int32),
                pltpu.SMEM((1, frames), jnp.int32),
                pltpu.SemaphoreType.DMA((3,)),
                pltpu.SemaphoreType.DMA((3, LOCAL)),
                pltpu.SemaphoreType.DMA((2, 2, LOCAL)),
                pltpu.SemaphoreType.DMA((2, 2, LOCAL)),
                pltpu.SemaphoreType.DMA,
                pltpu.SemaphoreType.DMA,
                pltpu.SemaphoreType.DMA((2,)),
                pltpu.SemaphoreType.REGULAR,
            ],
            compiler_params=pltpu.CompilerParams(
                collective_id=0, has_side_effects=True, vmem_limit_bytes=VMEM
            ),
        )(
            head_reach.T,
            frame_valid.reshape(1, frames),
            *(
                pltpu.with_memory_space_constraint(array.reshape(grid), pltpu.HBM)
                for array in (queries, keys, values)
            ),
        )
        return out.reshape(queries.shape)

    rows = P(("frame", "head"), None)
    return jax.shard_map(
        body, mesh=mesh, in_specs=(rows, rows, rows, P(), P()), out_specs=rows, check_vma=False
    )
```
